32 devices in a mesh: groups: 2 (over y), mz: 4 (over z), pix: 4 (over x, core).
Axes of the slice: x: 2, y: 2, z: 4, core: 2. Of those that a mesh axis runs over, the one named last changes fastest.
Arguments:
- spectra: bfloat16 [1024, 262144], P(('groups', 'pix'), 'mz'), parts along dimension 0
- kernel: bfloat16 [129], replicated, may hold values from 0.0009994507 to 0.029907227
- probes: bfloat16 [262144, 128], P('mz'), may hold values from -0.01171875 to 0.01171875
Outputs:
- basis: bfloat16 [1024, 128], P(('groups', 'pix')), parts along dimension 0
- projected: bfloat16 [256, 262144], P(('groups', 'pix'), 'mz'), parts along dimension 0
The draws below stay inside these ranges and needn't reach their ends.
There are 2 independent parts, one for each index of `groups`. The reference program is written for one: setup_inputs(seed, part) draws one part's arguments, and reference() takes and returns one part's arrays. A program takes and returns all parts, laid end to end along the dimension named above; an argument that names none is the same for every part. Nothing has to cross between parts.
All inputs are finite; a program needn't handle non-finite values.
Results may differ from the reference program's by a relative error of at most 0.019.
Values may be sent and summed in bfloat16 or wider, within the bound.
A program may use at most 192 MiB of HBM per device.

```python
import math
import jax
import jax.numpy as jnp
from jax import lax

BINS = 262144
PROBES = 128
BAND = 129
PIX_DEV = 128
PIXELS = 512
N_PIX = 4


def draw_spectra(key, part):
    first, second = jax.random.split(key, 2)
    phase = jax.random.uniform(second, (PIXELS, 1), jnp.float32) * 6.283
    position = jnp.arange(BINS, dtype=jnp.float32)[None, :]
    smooth = 1.5 + jnp.sin(position * (6.283 / 4096.0) + phase)
    rough = jax.random.normal(first, (PIXELS, BINS), jnp.float32)
    values = rough + smooth
    return values.astype(jnp.bfloat16)


def steps_of(rng, dims, cuts, low, high):
    def one(dim, shards_of):
        heights = jax.random.uniform(jax.random.fold_in(jax.random.fold_in(rng, 6), dim), (shards_of,), jnp.float32, low / len(cuts), high / len(cuts))
        return jnp.repeat(jnp.exp(heights), dims[dim] // shards_of).reshape((-1,) + (1,) * (len(dims) - dim - 1))

    factor_of = one(*cuts[0])
    for cut in cuts[1:]:
        factor_of = factor_of * one(*cut)
    return factor_of


def noise(stream_key, dims, width, bound, pieces=(), kind=jnp.bfloat16):
    values = width * jax.random.normal(stream_key, dims, jnp.float32)
    if pieces:
        values = values * steps_of(stream_key, dims, pieces, -0.22, 0.18)
    return jnp.clip(values, -bound, bound).astype(kind)


def setup_inputs(seed: int = 0, part: int = 0) -> dict:
    key_of = jax.random.split(jax.random.key(seed), 4)
    own_keys = jax.random.split(jax.random.fold_in(key_of[3], part), 4)
    spectra = draw_spectra(jax.random.fold_in(jax.random.fold_in(key_of[3], part), 71), part)
    kernel = jnp.clip(jnp.exp(jax.random.uniform(key_of[1], (BAND,), jnp.float32, math.log(0.0009994507), math.log(0.029907227))), 0.0009994507, 0.029907227).astype(jnp.bfloat16)
    probes = noise(key_of[2], (BINS, PROBES), BINS ** -0.5, 0.01171875, ((0, 4),))
    return {"spectra": spectra, "kernel": kernel, "probes": probes}


def smooth_block(rows, kernel):
    lhs = rows.astype(jnp.float32)[:, None, :]
    rhs = kernel.astype(jnp.float32)[None, None, :]
    base = lax.conv_general_dilated(lhs, rhs, (1,), ((64, 64),), dimension_numbers=('NCH', 'OIH', 'NCH'), precision=lax.Precision.HIGHEST)[:, 0, :]
    return (rows.astype(jnp.float32) - base).astype(jnp.bfloat16)

def reference(spectra, kernel, probes):
    blocks = spectra.reshape(N_PIX, PIX_DEV, BINS)
    cleaned_blocks = lax.map(lambda rows: smooth_block(rows, kernel), blocks)
    cleaned = cleaned_blocks.reshape(PIXELS, BINS)
    sketch = jnp.dot(cleaned.astype(jnp.float32), probes.astype(jnp.float32), preferred_element_type=jnp.float32)
    gram = jnp.dot(sketch.T, sketch, precision=lax.Precision.HIGHEST) / float(PIXELS)
    lower = jnp.linalg.cholesky(gram)
    basis_f = lax.linalg.triangular_solve(lower, sketch, left_side=False, lower=True, transpose_a=True)
    basis = basis_f.astype(jnp.bfloat16)
    factor = 1.0 / math.sqrt(float(PIXELS))
    total = jnp.zeros((PROBES, BINS), jnp.float32)
    for index in range(N_PIX):
        rows = basis[index * PIX_DEV:(index + 1) * PIX_DEV]
        part_sum = jnp.dot(rows.T.astype(jnp.float32), cleaned_blocks[index].astype(jnp.float32), preferred_element_type=jnp.float32) * factor
        total = total + part_sum.astype(jnp.bfloat16).astype(jnp.float32)
    return (basis, total.astype(jnp.bfloat16))
```

```python
import functools
import math

import jax
import jax.numpy as jnp
from jax import lax
from jax.experimental import pallas as pl
from jax.experimental.pallas import tpu as pltpu
from jax.sharding import PartitionSpec as P

LANES = 128
OUT = 256
WIN = OUT + 2 * LANES


MESH = pl.DeviceIdType.MESH
HIGHEST = lax.Precision.HIGHEST
PANEL = 8
EARLY = 5
AHEAD = 4
MET = 4


def whiten(a_ref, x_ref):
    size = a_ref.shape[0]
    row = lax.broadcasted_iota(jnp.int32, (PANEL, 1), 0)
    a = a_ref[...]
    x = (
        lax.broadcasted_iota(jnp.int32, (size, size), 0)
        == lax.broadcasted_iota(jnp.int32, (size, size), 1)
    ).astype(jnp.float32)
    blocks = size // PANEL
    a = [a[i * PANEL : (i + 1) * PANEL] for i in range(blocks)]
    x = [x[i * PANEL : (i + 1) * PANEL] for i in range(blocks)]
    for index in range(blocks):
        p, q = a[index], x[index]
        rows_p, rows_q = [], []
        spread = [
            jnp.broadcast_to(p[:, index * PANEL + t : index * PANEL + t + 1], p.shape)
            for t in range(PANEL)
        ]
        for t in range(PANEL):
            inv = lax.rsqrt(spread[t][t : t + 1])
            r, y = p[t : t + 1] * inv, q[t : t + 1] * inv
            rows_p.append(r)
            rows_q.append(y)
            if t + 1 < PANEL:
                scale = jnp.where(row > t, spread[t] * inv, 0.0)
                p = p - scale * r
                q = q - scale * y
                for j in range(t + 1, PANEL):
                    spread[j] = spread[j] - scale * (spread[j][t : t + 1] * inv)
        x_ref[index * PANEL : (index + 1) * PANEL, :] = jnp.concatenate(rows_q, axis=0)
        if index + 1 < blocks:
            turned = jnp.concatenate(rows_p, axis=0).T
            for later in range(index + 1, blocks):
                for t in range(PANEL):
                    scale = turned[later * PANEL : (later + 1) * PANEL, t : t + 1]
                    a[later] = a[later] - scale * rows_p[t]
                    x[later] = x[later] - scale * rows_q[t]


def fused_kernel(
    n_mz, n_pix, factor, pixels, early, ahead, spectra, k_ref, probes, basis, out,
    raw, tap, line, w_ref, halo, cleaned, total, parts, parts_in, sketch, gram, gram_in, x_ref,
    lhs, give, core_in, hold, x_give, x_in, acc, lhs_far, early_in, sketch_far,
    raw_sem, tap_sem, halo_send, halo_recv, parts_send, parts_recv, all_send, all_recv,
    gram_send, gram_recv, give_sem, core_sem, x_send_sem, x_recv_sem,
    early_send, early_recv, far_send, far_recv,
):
    bins = spectra.shape[1]
    slots, tile = tap.shape[0], tap.shape[1]
    tiles = bins // tile
    chips = n_pix // 2
    share = lhs.shape[0] // n_pix
    half = chips * share
    chunks, width = acc.shape[0], acc.shape[2]
    per = tile // width
    ring = give.shape[0]
    groups, mz, pix = lax.axis_index("groups"), lax.axis_index("mz"), lax.axis_index("pix")
    core = lax.rem(pix, 2)
    chip = lax.div(pix, 2)
    other = 1 - core

    def at_z(d):
        return (groups, lax.rem(mz + d, n_mz), pix)

    def at_pix(d):
        return (groups, mz, lax.rem(pix + d, n_pix))

    def device(at_chip, at_core):
        return (groups, mz, at_chip * 2 + at_core)

    def chip_of(d):
        return lax.rem(chip + d, chips)

    def tile_of(pos):
        return jnp.where(pos == tiles - 1, tiles - 1, jnp.where(pos == tiles - 2, 0, pos + 1))

    def each_load(pos, act):
        slot = lax.rem(pos, slots)

        @pl.when(pos < tiles - 2)
        def _():
            begin = pl.multiple_of((pos + 1) * tile - LANES, LANES)
            act(pltpu.make_async_copy(
                spectra.at[:, pl.ds(begin, tile + 2 * LANES)], raw.at[slot], raw_sem.at[slot]))

        @pl.when(pos == tiles - 2)
        def _():
            act(pltpu.make_async_copy(
                spectra.at[:, pl.ds(0, tile + LANES)],
                raw.at[slot, :, pl.ds(LANES, tile + LANES)], raw_sem.at[slot]))

        @pl.when(pos == tiles - 1)
        def _():
            act(pltpu.make_async_copy(
                spectra.at[:, pl.ds(bins - tile - LANES, tile + LANES)],
                raw.at[slot, :, pl.ds(0, tile + LANES)], raw_sem.at[slot]))

        begin = pl.multiple_of(tile_of(pos) * tile, tile)
        act(pltpu.make_async_copy(probes.at[pl.ds(begin, tile), :], tap.at[slot], tap_sem.at[slot]))

    both = chunks - 2 * early
    met = min(MET, tiles - 2)

    def whole_of(e, at_chip):
        return per + 2 * e + at_chip

    def chunk_of(i):
        return jnp.where(i < per, i, jnp.where(
            i < both, i + 2 * early, whole_of(i - both, chip)))

    def send_early(e):
        return pltpu.make_async_remote_copy(
            src_ref=cleaned.at[whole_of(e, 1 - chip)], dst_ref=early_in.at[e],
            send_sem=early_send.at[e], recv_sem=early_recv.at[e],
            device_id=device(1 - chip, core), device_id_type=MESH,
        )

    for pos in range(min(slots, tiles)):
        each_load(jnp.int32(pos), lambda c: c.start())

    barrier = pltpu.get_barrier_semaphore()
    for d in range(1, n_mz):
        pl.semaphore_signal(barrier, inc=1, device_id=at_z(d), device_id_type=MESH)
    for d in range(1, n_pix):
        pl.semaphore_signal(barrier, inc=1, device_id=at_pix(d), device_id_type=MESH)

    taps = k_ref.shape[0]
    line[...] = jnp.zeros_like(line)
    line[:, :taps] = k_ref[...].astype(jnp.float32).reshape(1, taps)
    base = jnp.broadcast_to(line[...], (OUT, WIN))
    band = pltpu.roll(base, LANES - taps // 2, 1, stride=1, stride_axis=0)
    w_ref[...] = band.T.astype(jnp.bfloat16)
    total[...] = jnp.zeros_like(total)

    to_right = pltpu.make_async_remote_copy(
        src_ref=spectra.at[:, pl.ds(bins - LANES, LANES)], dst_ref=halo.at[0],
        send_sem=halo_send.at[0], recv_sem=halo_recv.at[0],
        device_id=at_z(1), device_id_type=MESH,
    )
    to_left = pltpu.make_async_remote_copy(
        src_ref=spectra.at[:, pl.ds(0, LANES)], dst_ref=halo.at[1],
        send_sem=halo_send.at[1], recv_sem=halo_recv.at[1],
        device_id=at_z(n_mz - 1), device_id_type=MESH,
    )

    @pl.when(mz == 0)
    def _():
        halo[0] = jnp.zeros(halo.shape[1:], halo.dtype)

    @pl.when(mz == n_mz - 1)
    def _():
        halo[1] = jnp.zeros(halo.shape[1:], halo.dtype)

    def clean(pos):
        slot = lax.rem(pos, slots)
        at = tile_of(pos)
        each_load(pos, lambda c: c.wait())

        @pl.when(pos == tiles - 2)
        def _():
            @pl.when(mz > 0)
            def _():
                to_right.wait_recv()

            raw[slot, :, :LANES] = halo[0]

        @pl.when(pos == tiles - 1)
        def _():
            @pl.when(mz < n_mz - 1)
            def _():
                to_left.wait_recv()

            raw[slot, :, tile + LANES :] = halo[1]

        w = w_ref[...]
        done = []
        for j in range(tile // OUT):
            window = raw[slot, :, j * OUT : j * OUT + WIN]
            smooth = jnp.dot(window, w, preferred_element_type=jnp.float32)
            mine = raw[slot, :, LANES + j * OUT : LANES + (j + 1) * OUT].astype(jnp.float32)
            one = (mine - smooth).astype(jnp.bfloat16)
            piece, inside = (j * OUT) // width, (j * OUT) % width
            cleaned[at * per + piece, :, inside : inside + OUT] = one
            done.append(one)
        total[...] += jnp.dot(
            jnp.concatenate(done, axis=1), tap[slot], preferred_element_type=jnp.float32
        )

    @pl.loop(0, tiles)
    def _(pos):
        @pl.when(pos == met)
        def _():
            pl.semaphore_wait(barrier, n_mz - 1 + n_pix - 1)

            @pl.when(mz < n_mz - 1)
            def _():
                to_right.start()

            @pl.when(mz > 0)
            def _():
                to_left.start()

            for e in range(ahead):
                send_early(e).start()

        clean(pos)

        @pl.when(pos + slots < tiles)
        def _():
            each_load(pos + slots, lambda c: c.start())

    @pl.when(mz < n_mz - 1)
    def _():
        to_right.wait_send()

    @pl.when(mz > 0)
    def _():
        to_left.wait_send()

    rows = parts.shape[1]
    for z in range(n_mz):
        parts[z] = total[z * rows : (z + 1) * rows]

    def scatter(d):
        return pltpu.make_async_remote_copy(
            src_ref=parts.at[lax.rem(mz + d, n_mz)], dst_ref=parts_in.at[d - 1],
            send_sem=parts_send.at[d - 1], recv_sem=parts_recv.at[d - 1],
            device_id=at_z(d), device_id_type=MESH,
        )

    for d in range(1, n_mz):
        scatter(d).start()
    mine = parts[mz]
    for d in range(1, n_mz):
        scatter(d).wait_recv()
        mine = mine + parts_in[d - 1]
    sketch[mz] = mine

    def gather(d, owner):
        return pltpu.make_async_remote_copy(
            src_ref=sketch.at[mz], dst_ref=sketch.at[owner],
            send_sem=all_send.at[d - 1], recv_sem=all_recv.at[d - 1],
            device_id=at_z(d), device_id_type=MESH,
        )

    for d in range(1, n_mz):
        gather(d, mz).start()
    for d in range(1, n_mz):
        gather(d, lax.rem(mz + n_mz - d, n_mz)).wait_recv()
    sk = jnp.concatenate([sketch[z] for z in range(n_mz)], axis=0)

    gram[...] = lax.dot_general(
        sk, sk, (((0,), (0,)), ((), ())), precision=HIGHEST, preferred_element_type=jnp.float32
    )

    def share_gram(d):
        return pltpu.make_async_remote_copy(
            src_ref=gram, dst_ref=gram_in.at[d - 1],
            send_sem=gram_send.at[d - 1], recv_sem=gram_recv.at[d - 1],
            device_id=at_pix(d), device_id_type=MESH,
        )

    for d in range(1, n_pix):
        share_gram(d).start()
    to_far = pltpu.make_async_remote_copy(
        src_ref=sketch, dst_ref=sketch_far, send_sem=far_send.at[0], recv_sem=far_recv.at[0],
        device_id=device(1 - chip, core), device_id_type=MESH,
    )
    if early:
        to_far.start()
    full = gram[...]
    for d in range(1, n_pix):
        share_gram(d).wait_recv()
        full = full + gram_in[d - 1]
    if early:
        to_far.wait_recv()
        for e in range(ahead, early):
            send_early(e).start()
    total[...] = full * (1.0 / pixels)
    whiten(total, x_ref)
    x = x_ref[...]
    by_lane = (((1,), (1,)), ((), ()))

    def fill(target, of):
        flipped = lax.dot_general(
            x, of, by_lane, precision=HIGHEST, preferred_element_type=jnp.float32
        ).astype(jnp.bfloat16)
        basis_t = flipped.reshape(n_pix, share, flipped.shape[1])
        for chunk in range(n_pix):
            d = lax.rem(chunk // 2 - chip + chips, chips)
            at = d * share + jnp.where(core == chunk % 2, half, 0)
            target[pl.ds(pl.multiple_of(at, share), share), :] = basis_t[chunk]

    fill(lhs, sk)

    def to_core(k):
        return pltpu.make_async_remote_copy(
            src_ref=give.at[lax.rem(k, ring)], dst_ref=core_in.at[k],
            send_sem=give_sem.at[lax.rem(k, ring)], recv_sem=core_sem.at[k],
            device_id=device(chip, other), device_id_type=MESH,
        )

    def to_chip(d, k):
        return pltpu.make_async_remote_copy(
            src_ref=x_give.at[d - 1, k], dst_ref=x_in.at[d - 1, k],
            send_sem=x_send_sem.at[d - 1, k], recv_sem=x_recv_sem.at[d - 1, k],
            device_id=device(chip_of(d), core), device_id_type=MESH,
        )

    def product(left, right):
        part = jnp.dot(left, right, preferred_element_type=jnp.float32) * factor
        return part.astype(jnp.bfloat16)

    def first(i, alone):
        slot = lax.rem(i, ring)

        @pl.when(i >= ring)
        def _():
            to_core(i - ring).wait_send()

        part = product(lhs[...], cleaned[chunk_of(i)])
        if alone:
            send_early(i - both).wait_recv()
            far = product(lhs_far[...], early_in[i - both])
            part = (part.astype(jnp.float32) + far.astype(jnp.float32)).astype(jnp.bfloat16)
        give[slot] = part[:half]
        to_core(i).start()
        hold[slot] = part[half:]

    def second(i):
        to_core(i).wait_recv()
        slot = lax.rem(i, ring)
        k = chunk_of(i)
        added = hold[slot].astype(jnp.float32) + core_in[i].astype(jnp.float32)
        acc[k] = added[:share]
        for d in range(1, chips):
            x_give[d - 1, k] = added[d * share : (d + 1) * share].astype(jnp.bfloat16)
            to_chip(d, k).start()

    def emit(k, value):
        out[:, pl.ds(pl.multiple_of(k * width, width), width)] = value.astype(jnp.bfloat16)

    lag = min(ring - 1, both)
    mine = chunks - early

    @pl.loop(0, lag)
    def _(i):
        first(i, False)

    basis[...] = lax.dot_general(
        sk, x, by_lane, precision=HIGHEST, preferred_element_type=jnp.float32
    ).astype(jnp.bfloat16)

    @pl.loop(lag, both)
    def _(i):
        first(i, False)
        second(i - lag)

    if early:
        fill(lhs_far, jnp.concatenate([sketch_far[z] for z in range(n_mz)], axis=0))

        @pl.loop(both, mine)
        def _(i):
            first(i, True)
            second(i - lag)

    @pl.loop(mine - lag, mine)
    def _(i):
        second(i)

    @pl.loop(max(mine - ring, 0), mine)
    def _(i):
        to_core(i).wait_send()

    for d in range(1, n_mz):
        scatter(d).wait_send()
        gather(d, mz).wait_send()
    for d in range(1, n_pix):
        share_gram(d).wait_send()
    if early:
        to_far.wait_send()
        for e in range(early):
            send_early(e).wait_send()

        @pl.loop(0, early)
        def _(e):
            emit(whole_of(e, chip), acc[whole_of(e, chip)])

    @pl.loop(0, both)
    def _(i):
        k = chunk_of(i)
        added = acc[k]
        for d in range(1, chips):
            to_chip(d, k).wait()
            added = added + x_in[d - 1, k].astype(jnp.float32)
        emit(k, added)

    if early:
        @pl.loop(0, early)
        def _(e):
            k = whole_of(e, 1 - chip)
            to_chip(1, k).wait_recv()
            emit(k, x_in[0, k])
            to_chip(1, whole_of(e, chip)).wait_send()


def per_device(spectra, kernel, probes):
    rows, bins = spectra.shape
    cols = probes.shape[1]
    n_pix, n_mz = lax.axis_size("pix"), lax.axis_size("mz")
    pixels = rows * n_pix
    factor = 1.0 / math.sqrt(float(pixels))
    share = cols // n_pix
    chips = n_pix // 2
    half = chips * share
    tile = min(4096, bins // 2)
    width = min(1024, tile)
    chunks = bins // width
    slots, ring = 3, 4
    fits = chips == 2 and tile % width == 0 and bins // tile >= 8
    early, ahead = (EARLY, AHEAD) if fits else (0, 0)
    kept = max(early, 1)
    away = max(chips - 1, 1)
    part = rows // n_mz
    bf16, f32 = jnp.bfloat16, jnp.float32
    dma = pltpu.SemaphoreType.DMA
    return pl.pallas_call(
        functools.partial(fused_kernel, n_mz, n_pix, factor, float(pixels), early, ahead),
        in_specs=[
            pl.BlockSpec(memory_space=pl.ANY),
            pl.BlockSpec(memory_space=pltpu.VMEM),
            pl.BlockSpec(memory_space=pl.ANY),
        ],
        out_specs=[pl.BlockSpec(memory_space=pltpu.VMEM), pl.BlockSpec(memory_space=pltpu.VMEM)],
        out_shape=[
            pltpu.VMEM((rows, cols), bf16),
            pltpu.VMEM((share, bins), bf16),
        ],
        scratch_shapes=[
            pltpu.VMEM((slots, rows, tile + 2 * LANES), bf16),
            pltpu.VMEM((slots, tile, cols), bf16),
            pltpu.VMEM((1, WIN), f32),
            pltpu.VMEM((WIN, OUT), bf16),
            pltpu.VMEM((2, rows, LANES), bf16),
            pltpu.VMEM((chunks, rows, width), bf16),
            pltpu.VMEM((rows, cols), f32),
            pltpu.VMEM((n_mz, part, cols), f32),
            pltpu.VMEM((n_mz - 1, part, cols), f32),
            pltpu.VMEM((n_mz, part, cols), f32),
            pltpu.VMEM((cols, cols), f32),
            pltpu.VMEM((n_pix - 1, cols, cols), f32),
            pltpu.VMEM((cols, cols), f32),
            pltpu.VMEM((cols, rows), bf16),
            pltpu.VMEM((ring, half, width), bf16),
            pltpu.VMEM((chunks, half, width), bf16),
            pltpu.VMEM((ring, half, width), bf16),
            pltpu.VMEM((away, chunks, share, width), bf16),
            pltpu.VMEM((away, chunks, share, width), bf16),
            pltpu.VMEM((chunks, share, width), f32),
            pltpu.VMEM((cols, rows), bf16),
            pltpu.VMEM((kept, rows, width), bf16),
            pltpu.VMEM((n_mz, part, cols), f32),
            dma((slots,)),
            dma((slots,)),
            dma((2,)),
            dma((2,)),
            dma((n_mz - 1,)),
            dma((n_mz - 1,)),
            dma((n_mz - 1,)),
            dma((n_mz - 1,)),
            dma((n_pix - 1,)),
            dma((n_pix - 1,)),
            dma((ring,)),
            dma((chunks,)),
            dma((away, chunks)),
            dma((away, chunks)),
            dma((kept,)),
            dma((kept,)),
            dma((1,)),
            dma((1,)),
        ],
        compiler_params=pltpu.CompilerParams(
            collective_id=0, has_side_effects=True, vmem_limit_bytes=58 * 2**20
        ),
        cost_estimate=pl.CostEstimate(
            flops=2 * rows * bins * (WIN + 2 * cols),
            bytes_accessed=2 * bins * (rows + cols + share),
            transcendentals=0,
        ),
    )(spectra, kernel, probes)


def solution(mesh):
    in_specs = (P(("groups", "pix"), "mz"), P(), P("mz", None))
    out_specs = (P(("groups", "pix"), None), P(("groups", "pix"), "mz"))
    return jax.shard_map(
        per_device, mesh=mesh, in_specs=in_specs, out_specs=out_specs, check_vma=False
    )
```

```python
import functools
import math

import jax
import jax.numpy as jnp
from jax import lax
from jax.experimental import pallas as pl
from jax.experimental.pallas import tpu as pltpu
from jax.sharding import PartitionSpec as P

LANES = 128
OUT = 256
WIN = OUT + 2 * LANES


MESH = pl.DeviceIdType.MESH
HIGHEST = lax.Precision.HIGHEST
PANEL = 8
EARLY = 4
PIECES = 4
MARKS = (12, 13, 13, 16)
MET = 4


def whiten(a_ref, x_ref):
    size = a_ref.shape[0]
    row = lax.broadcasted_iota(jnp.int32, (PANEL, 1), 0)
    a = a_ref[...]
    x = (
        lax.broadcasted_iota(jnp.int32, (size, size), 0)
        == lax.broadcasted_iota(jnp.int32, (size, size), 1)
    ).astype(jnp.float32)
    blocks = size // PANEL
    a = [a[i * PANEL : (i + 1) * PANEL] for i in range(blocks)]
    x = [x[i * PANEL : (i + 1) * PANEL] for i in range(blocks)]
    for index in range(blocks):
        p, q = a[index], x[index]
        rows_p, rows_q = [], []
        spread = [
            jnp.broadcast_to(p[:, index * PANEL + t : index * PANEL + t + 1], p.shape)
            for t in range(PANEL)
        ]
        for t in range(PANEL):
            inv = lax.rsqrt(spread[t][t : t + 1])
            r, y = p[t : t + 1] * inv, q[t : t + 1] * inv
            rows_p.append(r)
            rows_q.append(y)
            if t + 1 < PANEL:
                scale = jnp.where(row > t, spread[t] * inv, 0.0)
                p = p - scale * r
                q = q - scale * y
                for j in range(t + 1, PANEL):
                    spread[j] = spread[j] - scale * (spread[j][t : t + 1] * inv)
        x_ref[index * PANEL : (index + 1) * PANEL, :] = jnp.concatenate(rows_q, axis=0)
        if index + 1 < blocks:
            turned = jnp.concatenate(rows_p, axis=0).T
            for later in range(index + 1, blocks):
                for t in range(PANEL):
                    scale = turned[later * PANEL : (later + 1) * PANEL, t : t + 1]
                    a[later] = a[later] - scale * rows_p[t]
                    x[later] = x[later] - scale * rows_q[t]


def write_kernel(basis, projected, basis_out, projected_out, sem):
    copies = [
        pltpu.make_async_copy(projected, projected_out, sem.at[0]),
        pltpu.make_async_copy(basis, basis_out, sem.at[1]),
    ]
    for copy in copies:
        copy.start()
    for copy in copies:
        copy.wait()


def fused_kernel(
    n_mz, n_pix, factor, pixels, early, marks, spectra, k_ref, probes, basis, out,
    raw, tap, line, w_ref, edge_ref, halo, cleaned, total, parts, parts_in, sketch, gram, gram_sum, gram_in, x_ref,
    lhs, give, core_in, hold, x_give, x_in, acc, lhs_far, early_in, sketch_far,
    raw_sem, tap_sem, halo_send, halo_recv, parts_send, parts_recv, all_send, all_recv,
    gram_send, gram_recv, give_sem, core_sem, x_send_sem, x_recv_sem,
    early_send, early_recv, far_send, far_recv,
):
    bins = spectra.shape[1]
    slots, tile = tap.shape[0], tap.shape[1]
    tiles = bins // tile
    chips = n_pix // 2
    share = lhs.shape[0] // n_pix
    half = chips * share
    chunks, width = acc.shape[0], acc.shape[2]
    per = tile // width
    ring = give.shape[0]
    groups, mz, pix = lax.axis_index("groups"), lax.axis_index("mz"), lax.axis_index("pix")
    core = lax.rem(pix, 2)
    chip = lax.div(pix, 2)
    other = 1 - core

    def at_z(d):
        return (groups, lax.rem(mz + d, n_mz), pix)

    def at_pix(d):
        return (groups, mz, lax.rem(pix + d, n_pix))

    def device(at_chip, at_core):
        return (groups, mz, at_chip * 2 + at_core)

    def chip_of(d):
        return lax.rem(chip + d, chips)

    def tile_of(pos):
        return jnp.where(pos == tiles - 1, tiles - 1, jnp.where(pos == tiles - 2, 0, pos + 1))

    def each_load(pos, act):
        slot = lax.rem(pos, slots)

        @pl.when(pos < tiles - 2)
        def _():
            begin = pl.multiple_of((pos + 1) * tile - LANES, LANES)
            act(pltpu.make_async_copy(
                spectra.at[:, pl.ds(begin, tile + 2 * LANES)], raw.at[slot], raw_sem.at[slot]))

        @pl.when(pos == tiles - 2)
        def _():
            act(pltpu.make_async_copy(
                spectra.at[:, pl.ds(0, tile + LANES)],
                raw.at[slot, :, pl.ds(LANES, tile + LANES)], raw_sem.at[slot]))

        @pl.when(pos == tiles - 1)
        def _():
            act(pltpu.make_async_copy(
                spectra.at[:, pl.ds(bins - tile - LANES, tile + LANES)],
                raw.at[slot, :, pl.ds(0, tile + LANES)], raw_sem.at[slot]))

        begin = pl.multiple_of(tile_of(pos) * tile, tile)
        act(pltpu.make_async_copy(probes.at[pl.ds(begin, tile), :], tap.at[slot], tap_sem.at[slot]))

    both = chunks - 2 * early
    met = min(MET, tiles - 2)

    def whole_of(e, at_chip):
        return per + 2 * e + at_chip

    def chunk_of(i):
        return jnp.where(i < per, i, jnp.where(
            i < both, i + 2 * early, whole_of(i - both, chip)))

    def send_early(i):
        e, piece = i // PIECES, i % PIECES
        size = early_in.shape[1] // PIECES
        at = pl.ds(piece * size, size)
        return pltpu.make_async_remote_copy(
            src_ref=cleaned.at[whole_of(e, 1 - chip), at], dst_ref=early_in.at[e, at],
            send_sem=early_send.at[i], recv_sem=early_recv.at[i],
            device_id=device(1 - chip, core), device_id_type=MESH,
        )

    def start_early(step):
        low, high = ((0,) + marks)[step : step + 2]
        for i in range(low, high):
            send_early(i).start()

    for pos in range(min(slots, tiles)):
        each_load(jnp.int32(pos), lambda c: c.start())

    barrier = pltpu.get_barrier_semaphore()
    for d in range(1, n_mz):
        pl.semaphore_signal(barrier, inc=1, device_id=at_z(d), device_id_type=MESH)
    for d in range(1, n_pix):
        pl.semaphore_signal(barrier, inc=1, device_id=at_pix(d), device_id_type=MESH)

    taps = k_ref.shape[0]
    line[...] = jnp.zeros_like(line)
    line[:, :taps] = k_ref[...].astype(jnp.float32).reshape(1, taps)
    base = jnp.broadcast_to(line[...], (OUT, WIN))
    band = pltpu.roll(base, LANES - taps // 2, 1, stride=1, stride_axis=0)
    full_band = band.T.astype(jnp.bfloat16)
    w_ref[...] = full_band[LANES : LANES + OUT]
    low = lax.broadcasted_iota(jnp.int32, (LANES, LANES), 0) < LANES // 2
    corner = jnp.where(low, full_band[WIN - LANES :, OUT - LANES :], full_band[:LANES, :LANES])
    edge_ref[...] = jnp.zeros_like(edge_ref)
    edge_ref[:LANES, :LANES] = corner
    edge_ref[LANES:, LANES:] = corner
    total[...] = jnp.zeros_like(total)

    to_right = pltpu.make_async_remote_copy(
        src_ref=spectra.at[:, pl.ds(bins - LANES, LANES)], dst_ref=halo.at[0],
        send_sem=halo_send.at[0], recv_sem=halo_recv.at[0],
        device_id=at_z(1), device_id_type=MESH,
    )
    to_left = pltpu.make_async_remote_copy(
        src_ref=spectra.at[:, pl.ds(0, LANES)], dst_ref=halo.at[1],
        send_sem=halo_send.at[1], recv_sem=halo_recv.at[1],
        device_id=at_z(n_mz - 1), device_id_type=MESH,
    )

    @pl.when(mz == 0)
    def _():
        halo[0] = jnp.zeros(halo.shape[1:], halo.dtype)

    @pl.when(mz == n_mz - 1)
    def _():
        halo[1] = jnp.zeros(halo.shape[1:], halo.dtype)

    def clean(pos):
        slot = lax.rem(pos, slots)
        at = tile_of(pos)
        each_load(pos, lambda c: c.wait())

        @pl.when(pos == tiles - 2)
        def _():
            @pl.when(mz > 0)
            def _():
                to_right.wait_recv()

            raw[slot, :, :LANES] = halo[0]

        @pl.when(pos == tiles - 1)
        def _():
            @pl.when(mz < n_mz - 1)
            def _():
                to_left.wait_recv()

            raw[slot, :, tile + LANES :] = halo[1]

        w, edge = w_ref[...], edge_ref[...]
        low = lax.broadcasted_iota(jnp.int32, (raw.shape[1], LANES), 1) < LANES // 2
        block = lambda i: raw[slot, :, LANES + i * LANES : LANES + (i + 1) * LANES]
        group = min(4, width // OUT)
        ready, added = [], None

        def sketch_part(js, added):
            begin, end = js[0] * OUT, (js[-1] + 1) * OUT
            piece, inside = begin // width, begin % width
            one = jnp.dot(
                cleaned[at * per + piece, :, inside : inside + end - begin],
                tap[slot, begin:end], preferred_element_type=jnp.float32,
            )
            return one if added is None else added + one

        for j in range(0, tile // OUT, 2):
            sides = [jnp.where(low, block(2 * k + 2), block(2 * k - 1)) for k in (j, j + 1)]
            outer = jnp.dot(
                jnp.concatenate(sides, axis=1), edge, preferred_element_type=jnp.float32
            )
            for k in (j, j + 1):
                mine = raw[slot, :, LANES + k * OUT : LANES + (k + 1) * OUT]
                inner = jnp.dot(mine, w, preferred_element_type=jnp.float32)
                side = outer[:, (k - j) * LANES : (k - j + 1) * LANES]
                smooth = inner + jnp.concatenate(
                    [jnp.where(low, side, 0.0), jnp.where(low, 0.0, side)], axis=1
                )
                one = (mine.astype(jnp.float32) - smooth).astype(jnp.bfloat16)
                piece, inside = (k * OUT) // width, (k * OUT) % width
                cleaned[at * per + piece, :, inside : inside + OUT] = one
            ready += [j, j + 1]
            if len(ready) >= 2 * group:
                added = sketch_part(ready[:group], added)
                ready = ready[group:]
        while ready:
            added = sketch_part(ready[:group], added)
            ready = ready[group:]
        total[...] += added

    @pl.loop(0, tiles)
    def _(pos):
        @pl.when(pos == met)
        def _():
            pl.semaphore_wait(barrier, n_mz - 1 + n_pix - 1)

            @pl.when(mz < n_mz - 1)
            def _():
                to_right.start()

            @pl.when(mz > 0)
            def _():
                to_left.start()

            start_early(0)

        clean(pos)

        @pl.when(pos + slots < tiles)
        def _():
            each_load(pos + slots, lambda c: c.start())

    @pl.when(mz < n_mz - 1)
    def _():
        to_right.wait_send()

    @pl.when(mz > 0)
    def _():
        to_left.wait_send()

    rows = parts.shape[1]
    for z in range(n_mz):
        parts[z] = total[z * rows : (z + 1) * rows]

    def scatter(d):
        return pltpu.make_async_remote_copy(
            src_ref=parts.at[lax.rem(mz + d, n_mz)], dst_ref=parts_in.at[d - 1],
            send_sem=parts_send.at[d - 1], recv_sem=parts_recv.at[d - 1],
            device_id=at_z(d), device_id_type=MESH,
        )

    for d in range(1, n_mz):
        scatter(d).start()
    start_early(1)
    mine = parts[mz]
    for d in range(1, n_mz):
        scatter(d).wait_recv()
        mine = mine + parts_in[d - 1]
    sketch[mz] = mine

    def gather(d, owner):
        return pltpu.make_async_remote_copy(
            src_ref=sketch.at[mz], dst_ref=sketch.at[owner],
            send_sem=all_send.at[d - 1], recv_sem=all_recv.at[d - 1],
            device_id=at_z(d), device_id_type=MESH,
        )

    for d in range(1, n_mz):
        gather(d, mz).start()
    start_early(2)
    for d in range(1, n_mz):
        gather(d, lax.rem(mz + n_mz - d, n_mz)).wait_recv()
    sk = jnp.concatenate([sketch[z] for z in range(n_mz)], axis=0)

    gram[...] = lax.dot_general(
        sk, sk, (((0,), (0,)), ((), ())), precision=HIGHEST, preferred_element_type=jnp.float32
    )

    def share_gram(d):
        return pltpu.make_async_remote_copy(
            src_ref=gram, dst_ref=gram_in.at[d - 1],
            send_sem=gram_send.at[d - 1], recv_sem=gram_recv.at[d - 1],
            device_id=device(chip_of(d), core), device_id_type=MESH,
        )

    relay = pltpu.make_async_remote_copy(
        src_ref=gram_sum, dst_ref=gram_in.at[chips - 1],
        send_sem=gram_send.at[chips - 1], recv_sem=gram_recv.at[chips - 1],
        device_id=device(chip, other), device_id_type=MESH,
    )

    for d in range(1, chips):
        share_gram(d).start()
    to_far = pltpu.make_async_remote_copy(
        src_ref=sketch, dst_ref=sketch_far, send_sem=far_send.at[0], recv_sem=far_recv.at[0],
        device_id=device(1 - chip, core), device_id_type=MESH,
    )
    if early:
        to_far.start()
    full = gram[...]
    for d in range(1, chips):
        share_gram(d).wait_recv()
        full = full + gram_in[d - 1]
    gram_sum[...] = full
    relay.start()
    relay.wait_recv()
    full = full + gram_in[chips - 1]
    if early:
        to_far.wait_recv()
        start_early(3)
    total[...] = full * (1.0 / pixels)
    whiten(total, x_ref)
    x = x_ref[...]
    by_lane = (((1,), (1,)), ((), ()))

    def fill(target, of):
        flipped = lax.dot_general(
            x, of, by_lane, precision=HIGHEST, preferred_element_type=jnp.float32
        ).astype(jnp.bfloat16)
        basis_t = flipped.reshape(n_pix, share, flipped.shape[1])
        for chunk in range(n_pix):
            d = lax.rem(chunk // 2 - chip + chips, chips)
            at = d * share + jnp.where(core == chunk % 2, half, 0)
            target[pl.ds(pl.multiple_of(at, share), share), :] = basis_t[chunk]

    fill(lhs, sk)

    def to_core(k):
        return pltpu.make_async_remote_copy(
            src_ref=give.at[lax.rem(k, ring)], dst_ref=core_in.at[k],
            send_sem=give_sem.at[lax.rem(k, ring)], recv_sem=core_sem.at[k],
            device_id=device(chip, other), device_id_type=MESH,
        )

    def to_chip(d, k):
        return pltpu.make_async_remote_copy(
            src_ref=x_give.at[d - 1, k], dst_ref=x_in.at[d - 1, k],
            send_sem=x_send_sem.at[d - 1, k], recv_sem=x_recv_sem.at[d - 1, k],
            device_id=device(chip_of(d), core), device_id_type=MESH,
        )

    def product(left, right):
        part = jnp.dot(left, right, preferred_element_type=jnp.float32) * factor
        return part.astype(jnp.bfloat16)

    def first(i, alone):
        slot = lax.rem(i, ring)

        @pl.when(i >= ring)
        def _():
            to_core(i - ring).wait_send()

        part = product(lhs[...], cleaned[chunk_of(i)])
        if alone:
            for piece in range(PIECES):
                send_early((i - both) * PIECES + piece).wait_recv()
            far = product(lhs_far[...], early_in[i - both])
            part = (part.astype(jnp.float32) + far.astype(jnp.float32)).astype(jnp.bfloat16)
        give[slot] = part[:half]
        to_core(i).start()
        hold[slot] = part[half:]

    def second(i):
        to_core(i).wait_recv()
        slot = lax.rem(i, ring)
        k = chunk_of(i)
        added = hold[slot].astype(jnp.float32) + core_in[i].astype(jnp.float32)
        acc[k] = added[:share]
        for d in range(1, chips):
            x_give[d - 1, k] = added[d * share : (d + 1) * share].astype(jnp.bfloat16)
            to_chip(d, k).start()

    def emit(k, value):
        out[:, pl.ds(pl.multiple_of(k * width, width), width)] = value.astype(jnp.bfloat16)

    lag = min(ring - 1, both)
    mine = chunks - early

    @pl.loop(0, lag)
    def _(i):
        first(i, False)

    basis[...] = lax.dot_general(
        sk, x, by_lane, precision=HIGHEST, preferred_element_type=jnp.float32
    ).astype(jnp.bfloat16)

    @pl.loop(lag, both)
    def _(i):
        first(i, False)
        second(i - lag)

    if early:
        fill(lhs_far, jnp.concatenate([sketch_far[z] for z in range(n_mz)], axis=0))

        @pl.loop(both, mine)
        def _(i):
            first(i, True)
            second(i - lag)

    @pl.loop(mine - lag, mine)
    def _(i):
        second(i)

    @pl.loop(max(mine - ring, 0), mine)
    def _(i):
        to_core(i).wait_send()

    for d in range(1, n_mz):
        scatter(d).wait_send()
        gather(d, mz).wait_send()
    for d in range(1, chips):
        share_gram(d).wait_send()
    relay.wait_send()
    if early:
        to_far.wait_send()
        for i in range(early * PIECES):
            send_early(i).wait_send()

        @pl.loop(0, early)
        def _(e):
            emit(whole_of(e, chip), acc[whole_of(e, chip)])

    @pl.loop(0, both)
    def _(i):
        k = chunk_of(i)
        added = acc[k]
        for d in range(1, chips):
            to_chip(d, k).wait()
            added = added + x_in[d - 1, k].astype(jnp.float32)
        emit(k, added)

    if early:
        @pl.loop(0, early)
        def _(e):
            k = whole_of(e, 1 - chip)
            to_chip(1, k).wait_recv()
            emit(k, x_in[0, k])
            to_chip(1, whole_of(e, chip)).wait_send()


def per_device(spectra, kernel, probes):
    rows, bins = spectra.shape
    cols = probes.shape[1]
    n_pix, n_mz = lax.axis_size("pix"), lax.axis_size("mz")
    pixels = rows * n_pix
    factor = 1.0 / math.sqrt(float(pixels))
    share = cols // n_pix
    chips = n_pix // 2
    half = chips * share
    tile = min(4096, bins // 2)
    width = min(1024, tile)
    chunks = bins // width
    slots, ring = 3, 4
    fits = chips == 2 and tile % width == 0 and bins // tile >= 8
    early, marks = (EARLY, MARKS) if fits else (0, (0, 0, 0, 0))
    kept = max(early, 1)
    away = max(chips - 1, 1)
    part = rows // n_mz
    bf16, f32 = jnp.bfloat16, jnp.float32
    dma = pltpu.SemaphoreType.DMA
    held = pl.pallas_call(
        functools.partial(fused_kernel, n_mz, n_pix, factor, float(pixels), early, marks),
        in_specs=[
            pl.BlockSpec(memory_space=pl.ANY),
            pl.BlockSpec(memory_space=pltpu.VMEM),
            pl.BlockSpec(memory_space=pl.ANY),
        ],
        out_specs=[pl.BlockSpec(memory_space=pltpu.VMEM), pl.BlockSpec(memory_space=pltpu.VMEM)],
        out_shape=[
            pltpu.VMEM((rows, cols), bf16),
            pltpu.VMEM((share, bins), bf16),
        ],
        scratch_shapes=[
            pltpu.VMEM((slots, rows, tile + 2 * LANES), bf16),
            pltpu.VMEM((slots, tile, cols), bf16),
            pltpu.VMEM((1, WIN), f32),
            pltpu.VMEM((OUT, OUT), bf16),
            pltpu.VMEM((OUT, OUT), bf16),
            pltpu.VMEM((2, rows, LANES), bf16),
            pltpu.VMEM((chunks, rows, width), bf16),
            pltpu.VMEM((rows, cols), f32),
            pltpu.VMEM((n_mz, part, cols), f32),
            pltpu.VMEM((n_mz - 1, part, cols), f32),
            pltpu.VMEM((n_mz, part, cols), f32),
            pltpu.VMEM((cols, cols), f32),
            pltpu.VMEM((cols, cols), f32),
            pltpu.VMEM((chips, cols, cols), f32),
            pltpu.VMEM((cols, cols), f32),
            pltpu.VMEM((cols, rows), bf16),
            pltpu.VMEM((ring, half, width), bf16),
            pltpu.VMEM((chunks, half, width), bf16),
            pltpu.VMEM((ring, half, width), bf16),
            pltpu.VMEM((away, chunks, share, width), bf16),
            pltpu.VMEM((away, chunks, share, width), bf16),
            pltpu.VMEM((chunks, share, width), f32),
            pltpu.VMEM((cols, rows), bf16),
            pltpu.VMEM((kept, rows, width), bf16),
            pltpu.VMEM((n_mz, part, cols), f32),
            dma((slots,)),
            dma((slots,)),
            dma((2,)),
            dma((2,)),
            dma((n_mz - 1,)),
            dma((n_mz - 1,)),
            dma((n_mz - 1,)),
            dma((n_mz - 1,)),
            dma((chips,)),
            dma((chips,)),
            dma((ring,)),
            dma((chunks,)),
            dma((away, chunks)),
            dma((away, chunks)),
            dma((kept * PIECES,)),
            dma((kept * PIECES,)),
            dma((1,)),
            dma((1,)),
        ],
        compiler_params=pltpu.CompilerParams(
            collective_id=0, has_side_effects=True, vmem_limit_bytes=58 * 2**20
        ),
        cost_estimate=pl.CostEstimate(
            flops=2 * rows * bins * (WIN + 2 * cols),
            bytes_accessed=2 * bins * (rows + cols + share),
            transcendentals=0,
        ),
    )(spectra, kernel, probes)
    return pl.pallas_call(
        write_kernel,
        in_specs=[pl.BlockSpec(memory_space=pltpu.VMEM)] * 2,
        out_specs=[pl.BlockSpec(memory_space=pl.ANY)] * 2,
        out_shape=[
            jax.ShapeDtypeStruct((rows, cols), bf16),
            jax.ShapeDtypeStruct((share, bins), bf16),
        ],
        scratch_shapes=[dma((2,))],
        compiler_params=pltpu.CompilerParams(vmem_limit_bytes=2**20),
    )(*[pltpu.with_memory_space_constraint(one, pltpu.VMEM) for one in held])


def solution(mesh):
    in_specs = (P(("groups", "pix"), "mz"), P(), P("mz", None))
    out_specs = (P(("groups", "pix"), None), P(("groups", "pix"), "mz"))
    return jax.shard_map(
        per_device, mesh=mesh, in_specs=in_specs, out_specs=out_specs, check_vma=False
    )
```

```python
import functools
import math

import jax
import jax.numpy as jnp
from jax import lax
from jax.experimental import pallas as pl
from jax.experimental.pallas import tpu as pltpu
from jax.sharding import PartitionSpec as P

LANES = 128
OUT = 256
WIN = OUT + 2 * LANES


MESH = pl.DeviceIdType.MESH
HIGHEST = lax.Precision.HIGHEST
PANEL = 16
PANELS = 4
EARLY = 4
PIECES = 4
MARKS = (13, 14, 14, 16)
MET = 4


def whiten(a_ref, x_ref):
    size = a_ref.shape[0]
    blocks = size // PANEL
    row = lax.broadcasted_iota(jnp.int32, (PANEL, 1), 0)
    a = a_ref[...]
    x = (
        lax.broadcasted_iota(jnp.int32, (size, size), 0)
        == lax.broadcasted_iota(jnp.int32, (size, size), 1)
    ).astype(jnp.float32)
    a = [a[i * PANEL : (i + 1) * PANEL] for i in range(blocks)]
    x = [x[i * PANEL : (i + 1) * PANEL] for i in range(blocks)]
    for index in range(blocks):
        base = index * PANEL
        first = index - index % PANELS
        last = min(first + PANELS, blocks)
        rows_a, rows_x = [], []
        spread = {
            i: [
                jnp.broadcast_to(a[i][:, base + t : base + t + 1], (PANEL, size))
                for t in range(PANEL)
            ]
            for i in range(index, last)
        }
        own = spread[index]
        for t in range(PANEL):
            inv = lax.rsqrt(own[t][t : t + 1])
            across = [own[j][t : t + 1] * inv for j in range(t + 1, PANEL)]
            r, y = a[index][t : t + 1] * inv, x[index][t : t + 1] * inv
            rows_a.append(r)
            rows_x.append(y)
            for i in range(index, last):
                scale = spread[i][t] * inv
                if i == index:
                    if t + 1 == PANEL:
                        continue
                    scale = jnp.where(row > t, scale, 0.0)
                for j in range(t + 1, PANEL):
                    spread[i][j] = spread[i][j] - scale * across[j - t - 1]
                a[i] = a[i] - scale * r
                x[i] = x[i] - scale * y
        a[index], x[index] = jnp.concatenate(rows_a, axis=0), jnp.concatenate(rows_x, axis=0)
        x_ref[base : base + PANEL, :] = x[index]
        if index + 1 == last and last < blocks:
            done = jnp.concatenate(a[first:last], axis=0)
            both = jnp.concatenate([done, jnp.concatenate(x[first:last], axis=0)], axis=1)
            minus = lax.dot_general(
                done, both, (((0,), (0,)), ((), ())), precision=HIGHEST,
                preferred_element_type=jnp.float32,
            )
            for later in range(last, blocks):
                rows = minus[later * PANEL : (later + 1) * PANEL]
                a[later] = a[later] - rows[:, :size]
                x[later] = x[later] - rows[:, size:]


def write_kernel(basis, projected, basis_out, projected_out, sem):
    copies = [
        pltpu.make_async_copy(projected, projected_out, sem.at[0]),
        pltpu.make_async_copy(basis, basis_out, sem.at[1]),
    ]
    for copy in copies:
        copy.start()
    for copy in copies:
        copy.wait()


def fused_kernel(
    n_mz, n_pix, factor, pixels, early, marks, spectra, k_ref, probes, basis, out,
    raw, tap, line, w_ref, edge_ref, halo, cleaned, total, parts, parts_in, sketch, gram, gram_sum, gram_in, x_ref,
    lhs, give, core_in, hold, x_give, x_in, acc, lhs_far, early_in, flat, flat_far,
    raw_sem, tap_sem, halo_send, halo_recv, parts_send, parts_recv, all_send, all_recv,
    gram_send, gram_recv, give_sem, core_sem, x_send_sem, x_recv_sem,
    early_send, early_recv, far_send, far_recv,
):
    bins = spectra.shape[1]
    slots, tile = tap.shape[0], tap.shape[1]
    tiles = bins // tile
    chips = n_pix // 2
    share = lhs.shape[0] // n_pix
    half = chips * share
    chunks, width = acc.shape[0], acc.shape[2]
    per = tile // width
    ring = give.shape[0]
    groups, mz, pix = lax.axis_index("groups"), lax.axis_index("mz"), lax.axis_index("pix")
    core = lax.rem(pix, 2)
    chip = lax.div(pix, 2)
    other = 1 - core

    def at_z(d):
        return (groups, lax.rem(mz + d, n_mz), pix)

    def at_pix(d):
        return (groups, mz, lax.rem(pix + d, n_pix))

    def device(at_chip, at_core):
        return (groups, mz, at_chip * 2 + at_core)

    def chip_of(d):
        return lax.rem(chip + d, chips)

    def tile_of(pos):
        return jnp.where(pos == tiles - 1, tiles - 1, jnp.where(pos == tiles - 2, 0, pos + 1))

    def each_load(pos, act):
        slot = lax.rem(pos, slots)

        @pl.when(pos < tiles - 2)
        def _():
            begin = pl.multiple_of((pos + 1) * tile - LANES, LANES)
            act(pltpu.make_async_copy(
                spectra.at[:, pl.ds(begin, tile + 2 * LANES)], raw.at[slot], raw_sem.at[slot]))

        @pl.when(pos == tiles - 2)
        def _():
            act(pltpu.make_async_copy(
                spectra.at[:, pl.ds(0, tile + LANES)],
                raw.at[slot, :, pl.ds(LANES, tile + LANES)], raw_sem.at[slot]))

        @pl.when(pos == tiles - 1)
        def _():
            act(pltpu.make_async_copy(
                spectra.at[:, pl.ds(bins - tile - LANES, tile + LANES)],
                raw.at[slot, :, pl.ds(0, tile + LANES)], raw_sem.at[slot]))

        begin = pl.multiple_of(tile_of(pos) * tile, tile)
        act(pltpu.make_async_copy(probes.at[pl.ds(begin, tile), :], tap.at[slot], tap_sem.at[slot]))

    both = chunks - 2 * early
    met = min(MET, tiles - 2)

    def whole_of(e, at_chip):
        return per + 2 * e + at_chip

    def chunk_of(i):
        return jnp.where(i < per, i, jnp.where(
            i < both, i + 2 * early, whole_of(i - both, chip)))

    def send_early(i):
        e, piece = i // PIECES, i % PIECES
        size = early_in.shape[1] // PIECES
        at = pl.ds(piece * size, size)
        return pltpu.make_async_remote_copy(
            src_ref=cleaned.at[whole_of(e, 1 - chip), at], dst_ref=early_in.at[e, at],
            send_sem=early_send.at[i], recv_sem=early_recv.at[i],
            device_id=device(1 - chip, core), device_id_type=MESH,
        )

    def start_early(step):
        low, high = ((0,) + marks)[step : step + 2]
        for i in range(low, high):
            send_early(i).start()

    each_load(jnp.int32(0), lambda c: c.start())

    barrier = pltpu.get_barrier_semaphore()
    for d in range(1, n_mz):
        pl.semaphore_signal(barrier, inc=1, device_id=at_z(d), device_id_type=MESH)
    for d in range(1, n_pix):
        pl.semaphore_signal(barrier, inc=1, device_id=at_pix(d), device_id_type=MESH)

    taps = k_ref.shape[0]
    line[...] = jnp.zeros_like(line)
    line[:, :taps] = k_ref[...].astype(jnp.float32).reshape(1, taps)
    base = jnp.broadcast_to(line[...], (OUT, WIN))
    band = pltpu.roll(base, LANES - taps // 2, 1, stride=1, stride_axis=0)
    full_band = band.T.astype(jnp.bfloat16)
    w_ref[...] = full_band[LANES : LANES + OUT]
    low = lax.broadcasted_iota(jnp.int32, (LANES, LANES), 0) < LANES // 2
    corner = jnp.where(low, full_band[WIN - LANES :, OUT - LANES :], full_band[:LANES, :LANES])
    edge_ref[...] = jnp.zeros_like(edge_ref)
    edge_ref[:LANES, :LANES] = corner
    edge_ref[LANES:, LANES:] = corner
    total[...] = jnp.zeros_like(total)
    for pos in range(1, min(slots, tiles)):
        each_load(jnp.int32(pos), lambda c: c.start())

    to_right = pltpu.make_async_remote_copy(
        src_ref=spectra.at[:, pl.ds(bins - LANES, LANES)], dst_ref=halo.at[0],
        send_sem=halo_send.at[0], recv_sem=halo_recv.at[0],
        device_id=at_z(1), device_id_type=MESH,
    )
    to_left = pltpu.make_async_remote_copy(
        src_ref=spectra.at[:, pl.ds(0, LANES)], dst_ref=halo.at[1],
        send_sem=halo_send.at[1], recv_sem=halo_recv.at[1],
        device_id=at_z(n_mz - 1), device_id_type=MESH,
    )

    @pl.when(mz == 0)
    def _():
        halo[0] = jnp.zeros(halo.shape[1:], halo.dtype)

    @pl.when(mz == n_mz - 1)
    def _():
        halo[1] = jnp.zeros(halo.shape[1:], halo.dtype)

    def clean(pos):
        slot = lax.rem(pos, slots)
        at = tile_of(pos)
        each_load(pos, lambda c: c.wait())

        @pl.when(pos == tiles - 2)
        def _():
            @pl.when(mz > 0)
            def _():
                to_right.wait_recv()

            raw[slot, :, :LANES] = halo[0]

        @pl.when(pos == tiles - 1)
        def _():
            @pl.when(mz < n_mz - 1)
            def _():
                to_left.wait_recv()

            raw[slot, :, tile + LANES :] = halo[1]

        w, edge = w_ref[...], edge_ref[...]
        low = lax.broadcasted_iota(jnp.int32, (raw.shape[1], LANES), 1) < LANES // 2
        block = lambda i: raw[slot, :, LANES + i * LANES : LANES + (i + 1) * LANES]
        group = 4
        ready, added = [], None

        def sketch_part(js, added):
            begin, end = js[0] * OUT, (js[-1] + 1) * OUT
            step = min(width, end - begin)
            pieces = [
                cleaned[at * per + i // width, :, i % width : i % width + step]
                for i in range(begin, end, step)
            ]
            one = jnp.dot(
                jnp.concatenate(pieces, axis=1), tap[slot, begin:end],
                preferred_element_type=jnp.float32,
            )
            return one if added is None else added + one

        for j in range(0, tile // OUT, 2):
            sides = [jnp.where(low, block(2 * k + 2), block(2 * k - 1)) for k in (j, j + 1)]
            outer = jnp.dot(
                jnp.concatenate(sides, axis=1), edge, preferred_element_type=jnp.float32
            )
            for k in (j, j + 1):
                mine = raw[slot, :, LANES + k * OUT : LANES + (k + 1) * OUT]
                inner = jnp.dot(mine, w, preferred_element_type=jnp.float32)
                side = outer[:, (k - j) * LANES : (k - j + 1) * LANES]
                smooth = inner + jnp.concatenate(
                    [jnp.where(low, side, 0.0), jnp.where(low, 0.0, side)], axis=1
                )
                one = (mine.astype(jnp.float32) - smooth).astype(jnp.bfloat16)
                piece, inside = (k * OUT) // width, (k * OUT) % width
                cleaned[at * per + piece, :, inside : inside + OUT] = one
            ready += [j, j + 1]
            if len(ready) >= 2 * group:
                added = sketch_part(ready[:group], added)
                ready = ready[group:]
        while ready:
            added = sketch_part(ready[:group], added)
            ready = ready[group:]
        total[...] += added

    @pl.loop(0, tiles)
    def _(pos):
        @pl.when(pos == met)
        def _():
            pl.semaphore_wait(barrier, n_mz - 1 + n_pix - 1)

            @pl.when(mz < n_mz - 1)
            def _():
                to_right.start()

            @pl.when(mz > 0)
            def _():
                to_left.start()

            start_early(0)

        clean(pos)

        @pl.when(pos + slots < tiles)
        def _():
            each_load(pos + slots, lambda c: c.start())

    @pl.when(mz < n_mz - 1)
    def _():
        to_right.wait_send()

    @pl.when(mz > 0)
    def _():
        to_left.wait_send()

    rows = parts.shape[1]
    for z in range(n_mz):
        parts[z] = total[z * rows : (z + 1) * rows]

    def scatter(d):
        return pltpu.make_async_remote_copy(
            src_ref=parts.at[lax.rem(mz + d, n_mz)], dst_ref=parts_in.at[d - 1],
            send_sem=parts_send.at[d - 1], recv_sem=parts_recv.at[d - 1],
            device_id=at_z(d), device_id_type=MESH,
        )

    for d in range(1, n_mz):
        scatter(d).start()
    start_early(1)
    mine = parts[mz]
    for d in range(1, n_mz):
        scatter(d).wait_recv()
        mine = mine + parts_in[d - 1]
    sketch[mz] = mine

    def gather(d, owner):
        return pltpu.make_async_remote_copy(
            src_ref=sketch.at[mz], dst_ref=sketch.at[owner],
            send_sem=all_send.at[d - 1], recv_sem=all_recv.at[d - 1],
            device_id=at_z(d), device_id_type=MESH,
        )

    for d in range(1, n_mz):
        gather(d, mz).start()
    start_early(2)
    for d in range(1, n_mz):
        gather(d, lax.rem(mz + n_mz - d, n_mz)).wait_recv()
    sk = jnp.concatenate([sketch[z] for z in range(n_mz)], axis=0)

    square = lax.dot_general(
        sk, sk, (((0,), (0,)), ((), ())), precision=HIGHEST, preferred_element_type=jnp.float32
    )
    size = square.shape[0]
    top, strip = size // 2, size // 4
    gram[:top] = square[:top]
    left = lax.broadcasted_iota(jnp.int32, (strip, size), 1) < top
    gram[top:] = jnp.where(
        left, pltpu.roll(square[top : top + strip], top, 1), square[top + strip :]
    )

    def share_gram(d):
        return pltpu.make_async_remote_copy(
            src_ref=gram, dst_ref=gram_in.at[d - 1],
            send_sem=gram_send.at[d - 1], recv_sem=gram_recv.at[d - 1],
            device_id=device(chip_of(d), core), device_id_type=MESH,
        )

    relay = pltpu.make_async_remote_copy(
        src_ref=gram_sum, dst_ref=gram_in.at[chips - 1],
        send_sem=gram_send.at[chips - 1], recv_sem=gram_recv.at[chips - 1],
        device_id=device(chip, other), device_id_type=MESH,
    )

    for d in range(1, chips):
        share_gram(d).start()
    to_far = pltpu.make_async_remote_copy(
        src_ref=flat, dst_ref=flat_far, send_sem=far_send.at[0], recv_sem=far_recv.at[0],
        device_id=device(1 - chip, core), device_id_type=MESH,
    )
    full = gram[...]
    for d in range(1, chips):
        share_gram(d).wait_recv()
        full = full + gram_in[d - 1]
    gram_sum[...] = full
    relay.start()
    relay.wait_recv()
    full = full + gram_in[chips - 1]
    if early:
        start_early(3)
    full = full * (1.0 / pixels)
    total[:top] = full[:top]
    total[top : top + strip] = pltpu.roll(full[top:], top, 1)
    total[top + strip :] = full[top:]
    whiten(total, x_ref)
    x = x_ref[...]
    by_lane = (((1,), (1,)), ((), ()))

    def fill(target, source):
        basis_t = source[...].reshape(n_pix, share, source.shape[1])
        for chunk in range(n_pix):
            d = lax.rem(chunk // 2 - chip + chips, chips)
            at = d * share + jnp.where(core == chunk % 2, half, 0)
            target[pl.ds(pl.multiple_of(at, share), share), :] = basis_t[chunk]

    flat[...] = lax.dot_general(
        x, sk, by_lane, precision=HIGHEST, preferred_element_type=jnp.float32
    ).astype(jnp.bfloat16)
    if early:
        to_far.start()
    fill(lhs, flat)

    def to_core(k):
        return pltpu.make_async_remote_copy(
            src_ref=give.at[lax.rem(k, ring)], dst_ref=core_in.at[k],
            send_sem=give_sem.at[lax.rem(k, ring)], recv_sem=core_sem.at[k],
            device_id=device(chip, other), device_id_type=MESH,
        )

    def to_chip(d, k):
        return pltpu.make_async_remote_copy(
            src_ref=x_give.at[d - 1, k], dst_ref=x_in.at[d - 1, k],
            send_sem=x_send_sem.at[d - 1, k], recv_sem=x_recv_sem.at[d - 1, k],
            device_id=device(chip_of(d), core), device_id_type=MESH,
        )

    def product(left, right):
        part = jnp.dot(left, right, preferred_element_type=jnp.float32) * factor
        return part.astype(jnp.bfloat16)

    def first(i, alone):
        slot = lax.rem(i, ring)

        @pl.when(i >= ring)
        def _():
            to_core(i - ring).wait_send()

        part = product(lhs[...], cleaned[chunk_of(i)])
        if alone:
            for piece in range(PIECES):
                send_early((i - both) * PIECES + piece).wait_recv()
            far = product(lhs_far[...], early_in[i - both])
            part = (part.astype(jnp.float32) + far.astype(jnp.float32)).astype(jnp.bfloat16)
        give[slot] = part[:half]
        to_core(i).start()
        hold[slot] = part[half:]

    def second(i):
        to_core(i).wait_recv()
        slot = lax.rem(i, ring)
        k = chunk_of(i)
        added = hold[slot].astype(jnp.float32) + core_in[i].astype(jnp.float32)
        acc[k] = added[:share]
        for d in range(1, chips):
            x_give[d - 1, k] = added[d * share : (d + 1) * share].astype(jnp.bfloat16)
            to_chip(d, k).start()

    def emit(k, value):
        out[:, pl.ds(pl.multiple_of(k * width, width), width)] = value.astype(jnp.bfloat16)

    lag = min(ring - 1, both)
    mine = chunks - early

    @pl.loop(0, lag)
    def _(i):
        first(i, False)

    @pl.loop(lag, both)
    def _(i):
        first(i, False)
        second(i - lag)

    basis[...] = lax.dot_general(
        sk, x, by_lane, precision=HIGHEST, preferred_element_type=jnp.float32
    ).astype(jnp.bfloat16)

    if early:
        to_far.wait_recv()
        fill(lhs_far, flat_far)

        @pl.loop(both, mine)
        def _(i):
            first(i, True)
            second(i - lag)

    @pl.loop(mine - lag, mine)
    def _(i):
        second(i)

    @pl.loop(max(mine - ring, 0), mine)
    def _(i):
        to_core(i).wait_send()

    for d in range(1, n_mz):
        scatter(d).wait_send()
        gather(d, mz).wait_send()
    for d in range(1, chips):
        share_gram(d).wait_send()
    relay.wait_send()
    if early:
        to_far.wait_send()
        for i in range(early * PIECES):
            send_early(i).wait_send()

        @pl.loop(0, early)
        def _(e):
            emit(whole_of(e, chip), acc[whole_of(e, chip)])

    @pl.loop(0, both)
    def _(i):
        k = chunk_of(i)
        added = acc[k]
        for d in range(1, chips):
            to_chip(d, k).wait()
            added = added + x_in[d - 1, k].astype(jnp.float32)
        emit(k, added)

    if early:
        @pl.loop(0, early)
        def _(e):
            k = whole_of(e, 1 - chip)
            to_chip(1, k).wait_recv()
            emit(k, x_in[0, k])
            to_chip(1, whole_of(e, chip)).wait_send()


def per_device(spectra, kernel, probes):
    rows, bins = spectra.shape
    cols = probes.shape[1]
    n_pix, n_mz = lax.axis_size("pix"), lax.axis_size("mz")
    pixels = rows * n_pix
    factor = 1.0 / math.sqrt(float(pixels))
    share = cols // n_pix
    chips = n_pix // 2
    half = chips * share
    tile = min(4096, bins // 2)
    width = min(1024, tile)
    chunks = bins // width
    slots, ring = 3, 4
    fits = chips == 2 and tile % width == 0 and bins // tile >= 8
    early, marks = (EARLY, MARKS) if fits else (0, (0, 0, 0, 0))
    kept = max(early, 1)
    away = max(chips - 1, 1)
    part = rows // n_mz
    bf16, f32 = jnp.bfloat16, jnp.float32
    dma = pltpu.SemaphoreType.DMA
    held = pl.pallas_call(
        functools.partial(fused_kernel, n_mz, n_pix, factor, float(pixels), early, marks),
        in_specs=[
            pl.BlockSpec(memory_space=pl.ANY),
            pl.BlockSpec(memory_space=pltpu.VMEM),
            pl.BlockSpec(memory_space=pl.ANY),
        ],
        out_specs=[pl.BlockSpec(memory_space=pltpu.VMEM), pl.BlockSpec(memory_space=pltpu.VMEM)],
        out_shape=[
            pltpu.VMEM((rows, cols), bf16),
            pltpu.VMEM((share, bins), bf16),
        ],
        scratch_shapes=[
            pltpu.VMEM((slots, rows, tile + 2 * LANES), bf16),
            pltpu.VMEM((slots, tile, cols), bf16),
            pltpu.VMEM((1, WIN), f32),
            pltpu.VMEM((OUT, OUT), bf16),
            pltpu.VMEM((OUT, OUT), bf16),
            pltpu.VMEM((2, rows, LANES), bf16),
            pltpu.VMEM((chunks, rows, width), bf16),
            pltpu.VMEM((rows, cols), f32),
            pltpu.VMEM((n_mz, part, cols), f32),
            pltpu.VMEM((n_mz - 1, part, cols), f32),
            pltpu.VMEM((n_mz, part, cols), f32),
            pltpu.VMEM((cols // 4 * 3, cols), f32),
            pltpu.VMEM((cols // 4 * 3, cols), f32),
            pltpu.VMEM((chips, cols // 4 * 3, cols), f32),
            pltpu.VMEM((cols, cols), f32),
            pltpu.VMEM((cols, rows), bf16),
            pltpu.VMEM((ring, half, width), bf16),
            pltpu.VMEM((chunks, half, width), bf16),
            pltpu.VMEM((ring, half, width), bf16),
            pltpu.VMEM((away, chunks, share, width), bf16),
            pltpu.VMEM((away, chunks, share, width), bf16),
            pltpu.VMEM((chunks, share, width), f32),
            pltpu.VMEM((cols, rows), bf16),
            pltpu.VMEM((kept, rows, width), bf16),
            pltpu.VMEM((cols, rows), bf16),
            pltpu.VMEM((cols, rows), bf16),
            dma((slots,)),
            dma((slots,)),
            dma((2,)),
            dma((2,)),
            dma((n_mz - 1,)),
            dma((n_mz - 1,)),
            dma((n_mz - 1,)),
            dma((n_mz - 1,)),
            dma((chips,)),
            dma((chips,)),
            dma((ring,)),
            dma((chunks,)),
            dma((away, chunks)),
            dma((away, chunks)),
            dma((kept * PIECES,)),
            dma((kept * PIECES,)),
            dma((1,)),
            dma((1,)),
        ],
        compiler_params=pltpu.CompilerParams(
            collective_id=0, has_side_effects=True, vmem_limit_bytes=58 * 2**20
        ),
        cost_estimate=pl.CostEstimate(
            flops=2 * rows * bins * (WIN + 2 * cols),
            bytes_accessed=2 * bins * (rows + cols + share),
            transcendentals=0,
        ),
    )(spectra, kernel, probes)
    return pl.pallas_call(
        write_kernel,
        in_specs=[pl.BlockSpec(memory_space=pltpu.VMEM)] * 2,
        out_specs=[pl.BlockSpec(memory_space=pl.ANY)] * 2,
        out_shape=[
            jax.ShapeDtypeStruct((rows, cols), bf16),
            jax.ShapeDtypeStruct((share, bins), bf16),
        ],
        scratch_shapes=[dma((2,))],
        compiler_params=pltpu.CompilerParams(vmem_limit_bytes=2**20),
    )(*[pltpu.with_memory_space_constraint(one, pltpu.VMEM) for one in held])


def solution(mesh):
    in_specs = (P(("groups", "pix"), "mz"), P(), P("mz", None))
    out_specs = (P(("groups", "pix"), None), P(("groups", "pix"), "mz"))
    return jax.shard_map(
        per_device, mesh=mesh, in_specs=in_specs, out_specs=out_specs, check_vma=False
    )
```

```python
import functools
import math

import jax
import jax.numpy as jnp
from jax import lax
from jax.experimental import pallas as pl
from jax.experimental.pallas import tpu as pltpu
from jax.sharding import PartitionSpec as P

LANES = 128
OUT = 256
WIN = OUT + 2 * LANES


MESH = pl.DeviceIdType.MESH
HIGHEST = lax.Precision.HIGHEST
PANEL = 16
PANELS = 4
EARLY = 2
LAG = 1
PIECES = 8
MARKS = (13, 14, 14, 16)
MET = 4


def whiten(a_ref, x_ref):
    size = a_ref.shape[0]
    blocks = size // PANEL
    row = lax.broadcasted_iota(jnp.int32, (PANEL, 1), 0)
    a = a_ref[...]
    x = (
        lax.broadcasted_iota(jnp.int32, (size, size), 0)
        == lax.broadcasted_iota(jnp.int32, (size, size), 1)
    ).astype(jnp.float32)
    a = [a[i * PANEL : (i + 1) * PANEL] for i in range(blocks)]
    x = [x[i * PANEL : (i + 1) * PANEL] for i in range(blocks)]
    for index in range(blocks):
        base = index * PANEL
        first = index - index % PANELS
        last = min(first + PANELS, blocks)
        rows_a, rows_x = [], []
        spread = {
            i: [
                jnp.broadcast_to(a[i][:, base + t : base + t + 1], (PANEL, size))
                for t in range(PANEL)
            ]
            for i in range(index, last)
        }
        own = spread[index]
        for t in range(PANEL):
            inv = lax.rsqrt(own[t][t : t + 1])
            across = [own[j][t : t + 1] * inv for j in range(t + 1, PANEL)]
            r, y = a[index][t : t + 1] * inv, x[index][t : t + 1] * inv
            rows_a.append(r)
            rows_x.append(y)
            for i in range(index, last):
                scale = spread[i][t] * inv
                if i == index:
                    if t + 1 == PANEL:
                        continue
                    scale = jnp.where(row > t, scale, 0.0)
                for j in range(t + 1, PANEL):
                    spread[i][j] = spread[i][j] - scale * across[j - t - 1]
                a[i] = a[i] - scale * r
                x[i] = x[i] - scale * y
        a[index], x[index] = jnp.concatenate(rows_a, axis=0), jnp.concatenate(rows_x, axis=0)
        x_ref[base : base + PANEL, :] = x[index]
        if index + 1 == last and last < blocks:
            done = jnp.concatenate(a[first:last], axis=0)
            both = jnp.concatenate([done, jnp.concatenate(x[first:last], axis=0)], axis=1)
            minus = lax.dot_general(
                done, both, (((0,), (0,)), ((), ())), precision=HIGHEST,
                preferred_element_type=jnp.float32,
            )
            for later in range(last, blocks):
                rows = minus[later * PANEL : (later + 1) * PANEL]
                a[later] = a[later] - rows[:, :size]
                x[later] = x[later] - rows[:, size:]


def write_kernel(basis, projected, basis_out, projected_out, sem):
    copies = [
        pltpu.make_async_copy(projected, projected_out, sem.at[0]),
        pltpu.make_async_copy(basis, basis_out, sem.at[1]),
    ]
    for copy in copies:
        copy.start()
    for copy in copies:
        copy.wait()


def fused_kernel(
    n_mz, n_pix, factor, pixels, early, marks, spectra, k_ref, probes, basis, out,
    raw, tap, line, w_ref, edge_ref, halo, cleaned, total, parts, parts_in, sketch, gram, gram_sum, gram_in, x_ref,
    lhs, give, core_in, hold, x_give, x_in, acc, lhs_far, early_in, flat, flat_far,
    raw_sem, tap_sem, halo_send, halo_recv, parts_send, parts_recv, all_send, all_recv,
    gram_send, gram_recv, give_sem, core_sem, x_send_sem, x_recv_sem,
    early_send, early_recv, far_send, far_recv,
):
    bins = spectra.shape[1]
    slots, tile = tap.shape[0], tap.shape[1]
    tiles = bins // tile
    chips = n_pix // 2
    share = lhs.shape[0] // n_pix
    half = chips * share
    chunks, width = acc.shape[0], acc.shape[2]
    per = tile // width
    ring = give.shape[0]
    groups, mz, pix = lax.axis_index("groups"), lax.axis_index("mz"), lax.axis_index("pix")
    core = lax.rem(pix, 2)
    chip = lax.div(pix, 2)
    other = 1 - core

    def at_z(d):
        return (groups, lax.rem(mz + d, n_mz), pix)

    def at_pix(d):
        return (groups, mz, lax.rem(pix + d, n_pix))

    def device(at_chip, at_core):
        return (groups, mz, at_chip * 2 + at_core)

    def chip_of(d):
        return lax.rem(chip + d, chips)

    def tile_of(pos):
        return jnp.where(pos == tiles - 1, tiles - 1, jnp.where(pos == tiles - 2, 0, pos + 1))

    def each_load(pos, act):
        slot = lax.rem(pos, slots)

        @pl.when(pos < tiles - 2)
        def _():
            begin = pl.multiple_of((pos + 1) * tile - LANES, LANES)
            act(pltpu.make_async_copy(
                spectra.at[:, pl.ds(begin, tile + 2 * LANES)], raw.at[slot], raw_sem.at[slot]))

        @pl.when(pos == tiles - 2)
        def _():
            act(pltpu.make_async_copy(
                spectra.at[:, pl.ds(0, tile + LANES)],
                raw.at[slot, :, pl.ds(LANES, tile + LANES)], raw_sem.at[slot]))

        @pl.when(pos == tiles - 1)
        def _():
            act(pltpu.make_async_copy(
                spectra.at[:, pl.ds(bins - tile - LANES, tile + LANES)],
                raw.at[slot, :, pl.ds(0, tile + LANES)], raw_sem.at[slot]))

        begin = pl.multiple_of(tile_of(pos) * tile, tile)
        act(pltpu.make_async_copy(probes.at[pl.ds(begin, tile), :], tap.at[slot], tap_sem.at[slot]))

    both = chunks - 2 * early
    met = min(MET, tiles - 2)

    def whole_of(e, at_chip):
        return per + 2 * e + at_chip

    def chunk_of(i):
        return jnp.where(i < per, i, jnp.where(
            i < both, i + 2 * early, whole_of(i - both, chip)))

    def send_early(i):
        e, piece = i // PIECES, i % PIECES
        size = early_in.shape[1] // PIECES
        at = pl.ds(piece * size, size)
        return pltpu.make_async_remote_copy(
            src_ref=cleaned.at[whole_of(e, 1 - chip), at], dst_ref=early_in.at[e, at],
            send_sem=early_send.at[i], recv_sem=early_recv.at[i],
            device_id=device(1 - chip, core), device_id_type=MESH,
        )

    def start_early(step):
        low, high = ((0,) + marks)[step : step + 2]
        for i in range(low, high):
            send_early(i).start()

    each_load(jnp.int32(0), lambda c: c.start())

    barrier = pltpu.get_barrier_semaphore()
    for d in range(1, n_mz):
        pl.semaphore_signal(barrier, inc=1, device_id=at_z(d), device_id_type=MESH)
    for d in range(1, n_pix):
        pl.semaphore_signal(barrier, inc=1, device_id=at_pix(d), device_id_type=MESH)

    taps = k_ref.shape[0]
    line[...] = jnp.zeros_like(line)
    line[:, :taps] = k_ref[...].astype(jnp.float32).reshape(1, taps)
    base = jnp.broadcast_to(line[...], (OUT, WIN))
    band = pltpu.roll(base, LANES - taps // 2, 1, stride=1, stride_axis=0)
    full_band = band.T.astype(jnp.bfloat16)
    w_ref[...] = full_band[LANES : LANES + OUT]
    low = lax.broadcasted_iota(jnp.int32, (LANES, LANES), 0) < LANES // 2
    corner = jnp.where(low, full_band[WIN - LANES :, OUT - LANES :], full_band[:LANES, :LANES])
    edge_ref[...] = jnp.zeros_like(edge_ref)
    edge_ref[:LANES, :LANES] = corner
    edge_ref[LANES:, LANES:] = corner
    total[...] = jnp.zeros_like(total)
    for pos in range(1, min(slots, tiles)):
        each_load(jnp.int32(pos), lambda c: c.start())

    to_right = pltpu.make_async_remote_copy(
        src_ref=spectra.at[:, pl.ds(bins - LANES, LANES)], dst_ref=halo.at[0],
        send_sem=halo_send.at[0], recv_sem=halo_recv.at[0],
        device_id=at_z(1), device_id_type=MESH,
    )
    to_left = pltpu.make_async_remote_copy(
        src_ref=spectra.at[:, pl.ds(0, LANES)], dst_ref=halo.at[1],
        send_sem=halo_send.at[1], recv_sem=halo_recv.at[1],
        device_id=at_z(n_mz - 1), device_id_type=MESH,
    )

    @pl.when(mz == 0)
    def _():
        halo[0] = jnp.zeros(halo.shape[1:], halo.dtype)

    @pl.when(mz == n_mz - 1)
    def _():
        halo[1] = jnp.zeros(halo.shape[1:], halo.dtype)

    def clean(pos):
        slot = lax.rem(pos, slots)
        at = tile_of(pos)
        each_load(pos, lambda c: c.wait())

        @pl.when(pos == tiles - 2)
        def _():
            @pl.when(mz > 0)
            def _():
                to_right.wait_recv()

            raw[slot, :, :LANES] = halo[0]

        @pl.when(pos == tiles - 1)
        def _():
            @pl.when(mz < n_mz - 1)
            def _():
                to_left.wait_recv()

            raw[slot, :, tile + LANES :] = halo[1]

        w, edge = w_ref[...], edge_ref[...]
        low = lax.broadcasted_iota(jnp.int32, (raw.shape[1], LANES), 1) < LANES // 2
        block = lambda i: raw[slot, :, LANES + i * LANES : LANES + (i + 1) * LANES]
        group = 4
        ready, added = [], None

        def sketch_part(js, added):
            begin, end = js[0] * OUT, (js[-1] + 1) * OUT
            step = min(width, end - begin)
            pieces = [
                cleaned[at * per + i // width, :, i % width : i % width + step]
                for i in range(begin, end, step)
            ]
            one = jnp.dot(
                jnp.concatenate(pieces, axis=1), tap[slot, begin:end],
                preferred_element_type=jnp.float32,
            )
            return one if added is None else added + one

        for j in range(0, tile // OUT, 2):
            sides = [jnp.where(low, block(2 * k + 2), block(2 * k - 1)) for k in (j, j + 1)]
            outer = jnp.dot(
                jnp.concatenate(sides, axis=1), edge, preferred_element_type=jnp.float32
            )
            for k in (j, j + 1):
                mine = raw[slot, :, LANES + k * OUT : LANES + (k + 1) * OUT]
                inner = jnp.dot(mine, w, preferred_element_type=jnp.float32)
                side = outer[:, (k - j) * LANES : (k - j + 1) * LANES]
                smooth = inner + jnp.concatenate(
                    [jnp.where(low, side, 0.0), jnp.where(low, 0.0, side)], axis=1
                )
                one = (mine.astype(jnp.float32) - smooth).astype(jnp.bfloat16)
                piece, inside = (k * OUT) // width, (k * OUT) % width
                cleaned[at * per + piece, :, inside : inside + OUT] = one
            ready += [j, j + 1]
            if len(ready) >= 2 * group:
                added = sketch_part(ready[:group], added)
                ready = ready[group:]
        while ready:
            added = sketch_part(ready[:group], added)
            ready = ready[group:]
        total[...] += added

    @pl.loop(0, tiles)
    def _(pos):
        @pl.when(pos == met)
        def _():
            pl.semaphore_wait(barrier, n_mz - 1 + n_pix - 1)

            @pl.when(mz < n_mz - 1)
            def _():
                to_right.start()

            @pl.when(mz > 0)
            def _():
                to_left.start()

            start_early(0)

        clean(pos)

        @pl.when(pos + slots < tiles)
        def _():
            each_load(pos + slots, lambda c: c.start())

    @pl.when(mz < n_mz - 1)
    def _():
        to_right.wait_send()

    @pl.when(mz > 0)
    def _():
        to_left.wait_send()

    rows = parts.shape[1]
    for z in range(n_mz):
        parts[z] = total[z * rows : (z + 1) * rows]

    def scatter(d):
        return pltpu.make_async_remote_copy(
            src_ref=parts.at[lax.rem(mz + d, n_mz)], dst_ref=parts_in.at[d - 1],
            send_sem=parts_send.at[d - 1], recv_sem=parts_recv.at[d - 1],
            device_id=at_z(d), device_id_type=MESH,
        )

    for d in range(1, n_mz):
        scatter(d).start()
    start_early(1)
    mine = parts[mz]
    for d in range(1, n_mz):
        scatter(d).wait_recv()
        mine = mine + parts_in[d - 1]
    sketch[mz] = mine

    def gather(d, owner):
        return pltpu.make_async_remote_copy(
            src_ref=sketch.at[mz], dst_ref=sketch.at[owner],
            send_sem=all_send.at[d - 1], recv_sem=all_recv.at[d - 1],
            device_id=at_z(d), device_id_type=MESH,
        )

    for d in range(1, n_mz):
        gather(d, mz).start()
    start_early(2)
    for d in range(1, n_mz):
        gather(d, lax.rem(mz + n_mz - d, n_mz)).wait_recv()
    sk = jnp.concatenate([sketch[z] for z in range(n_mz)], axis=0)

    square = lax.dot_general(
        sk, sk, (((0,), (0,)), ((), ())), precision=HIGHEST, preferred_element_type=jnp.float32
    )
    size = square.shape[0]
    top, strip = size // 2, size // 4
    gram[:top] = square[:top]
    left = lax.broadcasted_iota(jnp.int32, (strip, size), 1) < top
    gram[top:] = jnp.where(
        left, pltpu.roll(square[top : top + strip], top, 1), square[top + strip :]
    )

    def share_gram(d):
        return pltpu.make_async_remote_copy(
            src_ref=gram, dst_ref=gram_in.at[d - 1],
            send_sem=gram_send.at[d - 1], recv_sem=gram_recv.at[d - 1],
            device_id=device(chip_of(d), core), device_id_type=MESH,
        )

    relay = pltpu.make_async_remote_copy(
        src_ref=gram_sum, dst_ref=gram_in.at[chips - 1],
        send_sem=gram_send.at[chips - 1], recv_sem=gram_recv.at[chips - 1],
        device_id=device(chip, other), device_id_type=MESH,
    )

    for d in range(1, chips):
        share_gram(d).start()
    to_far = pltpu.make_async_remote_copy(
        src_ref=flat, dst_ref=flat_far, send_sem=far_send.at[0], recv_sem=far_recv.at[0],
        device_id=device(1 - chip, core), device_id_type=MESH,
    )
    full = gram[...]
    for d in range(1, chips):
        share_gram(d).wait_recv()
        full = full + gram_in[d - 1]
    gram_sum[...] = full
    relay.start()
    relay.wait_recv()
    full = full + gram_in[chips - 1]
    if early:
        start_early(3)
    full = full * (1.0 / pixels)
    total[:top] = full[:top]
    total[top : top + strip] = pltpu.roll(full[top:], top, 1)
    total[top + strip :] = full[top:]
    whiten(total, x_ref)
    x = x_ref[...]
    by_lane = (((1,), (1,)), ((), ()))

    def fill(target, source):
        basis_t = source[...].reshape(n_pix, share, source.shape[1])
        for chunk in range(n_pix):
            d = lax.rem(chunk // 2 - chip + chips, chips)
            at = d * share + jnp.where(core == chunk % 2, half, 0)
            target[pl.ds(pl.multiple_of(at, share), share), :] = basis_t[chunk]

    flat[...] = lax.dot_general(
        x, sk, by_lane, precision=HIGHEST, preferred_element_type=jnp.float32
    ).astype(jnp.bfloat16)
    if early:
        to_far.start()
    fill(lhs, flat)

    def to_core(k):
        return pltpu.make_async_remote_copy(
            src_ref=give.at[lax.rem(k, ring)], dst_ref=core_in.at[k],
            send_sem=give_sem.at[lax.rem(k, ring)], recv_sem=core_sem.at[k],
            device_id=device(chip, other), device_id_type=MESH,
        )

    def to_chip(d, k):
        return pltpu.make_async_remote_copy(
            src_ref=x_give.at[d - 1, k], dst_ref=x_in.at[d - 1, k],
            send_sem=x_send_sem.at[d - 1, k], recv_sem=x_recv_sem.at[d - 1, k],
            device_id=device(chip_of(d), core), device_id_type=MESH,
        )

    def product(left, right):
        part = jnp.dot(left, right, preferred_element_type=jnp.float32) * factor
        return part.astype(jnp.bfloat16)

    def first(i, alone):
        slot = lax.rem(i, ring)

        @pl.when(i >= ring)
        def _():
            to_core(i - ring).wait_send()

        part = product(lhs[...], cleaned[chunk_of(i)])
        if alone:
            for piece in range(PIECES):
                send_early((i - both) * PIECES + piece).wait_recv()
            far = product(lhs_far[...], early_in[i - both])
            part = (part.astype(jnp.float32) + far.astype(jnp.float32)).astype(jnp.bfloat16)
        give[slot] = part[:half]
        to_core(i).start()
        hold[slot] = part[half:]

    def second(i):
        to_core(i).wait_recv()
        slot = lax.rem(i, ring)
        k = chunk_of(i)
        added = hold[slot].astype(jnp.float32) + core_in[i].astype(jnp.float32)
        acc[k] = added[:share]
        for d in range(1, chips):
            x_give[d - 1, k] = added[d * share : (d + 1) * share].astype(jnp.bfloat16)
            to_chip(d, k).start()

    def emit(k, value):
        out[:, pl.ds(pl.multiple_of(k * width, width), width)] = value.astype(jnp.bfloat16)

    lag = min(LAG, ring - 1, both)
    mine = chunks - early

    @pl.loop(0, lag)
    def _(i):
        first(i, False)

    @pl.loop(lag, both)
    def _(i):
        first(i, False)
        second(i - lag)

    basis[...] = lax.dot_general(
        sk, x, by_lane, precision=HIGHEST, preferred_element_type=jnp.float32
    ).astype(jnp.bfloat16)

    if early:
        to_far.wait_recv()
        fill(lhs_far, flat_far)

        @pl.loop(both, mine)
        def _(i):
            first(i, True)
            second(i - lag)

    @pl.loop(mine - lag, mine)
    def _(i):
        second(i)

    @pl.loop(max(mine - ring, 0), mine)
    def _(i):
        to_core(i).wait_send()

    for d in range(1, n_mz):
        scatter(d).wait_send()
        gather(d, mz).wait_send()
    for d in range(1, chips):
        share_gram(d).wait_send()
    relay.wait_send()
    if early:
        to_far.wait_send()
        for i in range(early * PIECES):
            send_early(i).wait_send()

        @pl.loop(0, early)
        def _(e):
            emit(whole_of(e, chip), acc[whole_of(e, chip)])

    @pl.loop(0, both)
    def _(i):
        k = chunk_of(i)
        added = acc[k]
        for d in range(1, chips):
            to_chip(d, k).wait()
            added = added + x_in[d - 1, k].astype(jnp.float32)
        emit(k, added)

    if early:
        @pl.loop(0, early)
        def _(e):
            k = whole_of(e, 1 - chip)
            to_chip(1, k).wait_recv()
            emit(k, x_in[0, k])
            to_chip(1, whole_of(e, chip)).wait_send()


def per_device(spectra, kernel, probes):
    rows, bins = spectra.shape
    cols = probes.shape[1]
    n_pix, n_mz = lax.axis_size("pix"), lax.axis_size("mz")
    pixels = rows * n_pix
    factor = 1.0 / math.sqrt(float(pixels))
    share = cols // n_pix
    chips = n_pix // 2
    half = chips * share
    tile = min(4096, bins // 2)
    width = min(2048, tile)
    chunks = bins // width
    slots, ring = 3, 4
    fits = chips == 2 and tile % width == 0 and bins // tile >= 8
    early, marks = (EARLY, MARKS) if fits else (0, (0, 0, 0, 0))
    kept = max(early, 1)
    away = max(chips - 1, 1)
    part = rows // n_mz
    bf16, f32 = jnp.bfloat16, jnp.float32
    dma = pltpu.SemaphoreType.DMA
    held = pl.pallas_call(
        functools.partial(fused_kernel, n_mz, n_pix, factor, float(pixels), early, marks),
        in_specs=[
            pl.BlockSpec(memory_space=pl.ANY),
            pl.BlockSpec(memory_space=pltpu.VMEM),
            pl.BlockSpec(memory_space=pl.ANY),
        ],
        out_specs=[pl.BlockSpec(memory_space=pltpu.VMEM), pl.BlockSpec(memory_space=pltpu.VMEM)],
        out_shape=[
            pltpu.VMEM((rows, cols), bf16),
            pltpu.VMEM((share, bins), bf16),
        ],
        scratch_shapes=[
            pltpu.VMEM((slots, rows, tile + 2 * LANES), bf16),
            pltpu.VMEM((slots, tile, cols), bf16),
            pltpu.VMEM((1, WIN), f32),
            pltpu.VMEM((OUT, OUT), bf16),
            pltpu.VMEM((OUT, OUT), bf16),
            pltpu.VMEM((2, rows, LANES), bf16),
            pltpu.VMEM((chunks, rows, width), bf16),
            pltpu.VMEM((rows, cols), f32),
            pltpu.VMEM((n_mz, part, cols), f32),
            pltpu.VMEM((n_mz - 1, part, cols), f32),
            pltpu.VMEM((n_mz, part, cols), f32),
            pltpu.VMEM((cols // 4 * 3, cols), f32),
            pltpu.VMEM((cols // 4 * 3, cols), f32),
            pltpu.VMEM((chips, cols // 4 * 3, cols), f32),
            pltpu.VMEM((cols, cols), f32),
            pltpu.VMEM((cols, rows), bf16),
            pltpu.VMEM((ring, half, width), bf16),
            pltpu.VMEM((chunks, half, width), bf16),
            pltpu.VMEM((ring, half, width), bf16),
            pltpu.VMEM((away, chunks, share, width), bf16),
            pltpu.VMEM((away, chunks, share, width), bf16),
            pltpu.VMEM((chunks, share, width), f32),
            pltpu.VMEM((cols, rows), bf16),
            pltpu.VMEM((kept, rows, width), bf16),
            pltpu.VMEM((cols, rows), bf16),
            pltpu.VMEM((cols, rows), bf16),
            dma((slots,)),
            dma((slots,)),
            dma((2,)),
            dma((2,)),
            dma((n_mz - 1,)),
            dma((n_mz - 1,)),
            dma((n_mz - 1,)),
            dma((n_mz - 1,)),
            dma((chips,)),
            dma((chips,)),
            dma((ring,)),
            dma((chunks,)),
            dma((away, chunks)),
            dma((away, chunks)),
            dma((kept * PIECES,)),
            dma((kept * PIECES,)),
            dma((1,)),
            dma((1,)),
        ],
        compiler_params=pltpu.CompilerParams(
            collective_id=0, has_side_effects=True, vmem_limit_bytes=58 * 2**20
        ),
        cost_estimate=pl.CostEstimate(
            flops=2 * rows * bins * (WIN + 2 * cols),
            bytes_accessed=2 * bins * (rows + cols + share),
            transcendentals=0,
        ),
    )(spectra, kernel, probes)
    return pl.pallas_call(
        write_kernel,
        in_specs=[pl.BlockSpec(memory_space=pltpu.VMEM)] * 2,
        out_specs=[pl.BlockSpec(memory_space=pl.ANY)] * 2,
        out_shape=[
            jax.ShapeDtypeStruct((rows, cols), bf16),
            jax.ShapeDtypeStruct((share, bins), bf16),
        ],
        scratch_shapes=[dma((2,))],
        compiler_params=pltpu.CompilerParams(vmem_limit_bytes=2**20),
    )(*[pltpu.with_memory_space_constraint(one, pltpu.VMEM) for one in held])


def solution(mesh):
    in_specs = (P(("groups", "pix"), "mz"), P(), P("mz", None))
    out_specs = (P(("groups", "pix"), None), P(("groups", "pix"), "mz"))
    return jax.shard_map(
        per_device, mesh=mesh, in_specs=in_specs, out_specs=out_specs, check_vma=False
    )
```

```python
import functools
import math

import jax
import jax.numpy as jnp
from jax import lax
from jax.experimental import pallas as pl
from jax.experimental.pallas import tpu as pltpu
from jax.sharding import PartitionSpec as P

LANES = 128
OUT = 256
WIN = OUT + 2 * LANES


MESH = pl.DeviceIdType.MESH
HIGHEST = lax.Precision.HIGHEST
PANEL = 16
PANELS = 4
EARLY = 2
LAG = 1
PIECES = 4
MARKS = (7, 7, 7, 8)
MET = 4


def whiten(a_ref, x_ref):
    size = a_ref.shape[0]
    blocks = size // PANEL
    row = lax.broadcasted_iota(jnp.int32, (PANEL, 1), 0)
    a = a_ref[...]
    x = (
        lax.broadcasted_iota(jnp.int32, (size, size), 0)
        == lax.broadcasted_iota(jnp.int32, (size, size), 1)
    ).astype(jnp.float32)
    a = [a[i * PANEL : (i + 1) * PANEL] for i in range(blocks)]
    x = [x[i * PANEL : (i + 1) * PANEL] for i in range(blocks)]
    for index in range(blocks):
        base = index * PANEL
        first = index - index % PANELS
        last = min(first + PANELS, blocks)
        rows_a, rows_x = [], []
        spread = {
            i: [
                jnp.broadcast_to(a[i][:, base + t : base + t + 1], (PANEL, size))
                for t in range(PANEL)
            ]
            for i in range(index, last)
        }
        own = spread[index]
        for t in range(PANEL):
            inv = lax.rsqrt(own[t][t : t + 1])
            across = [own[j][t : t + 1] * inv for j in range(t + 1, PANEL)]
            r, y = a[index][t : t + 1] * inv, x[index][t : t + 1] * inv
            rows_a.append(r)
            rows_x.append(y)
            for i in range(index, last):
                scale = spread[i][t] * inv
                if i == index:
                    if t + 1 == PANEL:
                        continue
                    scale = jnp.where(row > t, scale, 0.0)
                for j in range(t + 1, PANEL):
                    spread[i][j] = spread[i][j] - scale * across[j - t - 1]
                a[i] = a[i] - scale * r
                x[i] = x[i] - scale * y
        a[index], x[index] = jnp.concatenate(rows_a, axis=0), jnp.concatenate(rows_x, axis=0)
        x_ref[base : base + PANEL, :] = x[index]
        if index + 1 == last and last < blocks:
            done = jnp.concatenate(a[first:last], axis=0)
            both = jnp.concatenate([done, jnp.concatenate(x[first:last], axis=0)], axis=1)
            minus = lax.dot_general(
                done, both, (((0,), (0,)), ((), ())), precision=HIGHEST,
                preferred_element_type=jnp.float32,
            )
            for later in range(last, blocks):
                rows = minus[later * PANEL : (later + 1) * PANEL]
                a[later] = a[later] - rows[:, :size]
                x[later] = x[later] - rows[:, size:]


def write_kernel(basis, projected, basis_out, projected_out, sem):
    copies = [
        pltpu.make_async_copy(projected, projected_out, sem.at[0]),
        pltpu.make_async_copy(basis, basis_out, sem.at[1]),
    ]
    for copy in copies:
        copy.start()
    for copy in copies:
        copy.wait()


def fused_kernel(
    n_mz, n_pix, factor, pixels, early, marks, spectra, k_ref, probes, basis, out,
    raw, tap, line, w_ref, edge_ref, halo, cleaned, total, parts, parts_in, sketch, gram, gram_sum, gram_in, x_ref,
    lhs, give, core_in, hold, x_give, x_in, acc, lhs_far, early_in, flat, flat_far,
    raw_sem, tap_sem, halo_send, halo_recv, parts_send, parts_recv, all_send, all_recv,
    gram_send, gram_recv, give_sem, core_sem, x_send_sem, x_recv_sem,
    early_send, early_recv, far_send, far_recv,
):
    bins = spectra.shape[1]
    slots, tile = tap.shape[0], tap.shape[1]
    tiles = bins // tile
    chips = n_pix // 2
    share = lhs.shape[0] // n_pix
    half = chips * share
    chunks, width = acc.shape[0], acc.shape[2]
    per = tile // width
    ring = give.shape[0]
    groups, mz, pix = lax.axis_index("groups"), lax.axis_index("mz"), lax.axis_index("pix")
    core = lax.rem(pix, 2)
    chip = lax.div(pix, 2)
    other = 1 - core

    def at_z(d):
        return (groups, lax.rem(mz + d, n_mz), pix)

    def at_pix(d):
        return (groups, mz, lax.rem(pix + d, n_pix))

    def device(at_chip, at_core):
        return (groups, mz, at_chip * 2 + at_core)

    def chip_of(d):
        return lax.rem(chip + d, chips)

    def tile_of(pos):
        return jnp.where(pos == tiles - 1, tiles - 1, jnp.where(pos == tiles - 2, 0, pos + 1))

    def each_load(pos, act):
        slot = lax.rem(pos, slots)

        @pl.when(pos < tiles - 2)
        def _():
            begin = pl.multiple_of((pos + 1) * tile - LANES, LANES)
            act(pltpu.make_async_copy(
                spectra.at[:, pl.ds(begin, tile + 2 * LANES)], raw.at[slot], raw_sem.at[slot]))

        @pl.when(pos == tiles - 2)
        def _():
            act(pltpu.make_async_copy(
                spectra.at[:, pl.ds(0, tile + LANES)],
                raw.at[slot, :, pl.ds(LANES, tile + LANES)], raw_sem.at[slot]))

        @pl.when(pos == tiles - 1)
        def _():
            act(pltpu.make_async_copy(
                spectra.at[:, pl.ds(bins - tile - LANES, tile + LANES)],
                raw.at[slot, :, pl.ds(0, tile + LANES)], raw_sem.at[slot]))

        begin = pl.multiple_of(tile_of(pos) * tile, tile)
        act(pltpu.make_async_copy(probes.at[pl.ds(begin, tile), :], tap.at[slot], tap_sem.at[slot]))

    both = chunks - 2 * early
    met = min(MET, tiles - 2)

    def whole_of(e, at_chip):
        return per + 2 * e + at_chip

    def chunk_of(i):
        return jnp.where(i < per, i, jnp.where(
            i < both, i + 2 * early, whole_of(i - both, chip)))

    def send_early(i):
        e, piece = i // PIECES, i % PIECES
        size = early_in.shape[1] // PIECES
        at = pl.ds(piece * size, size)
        return pltpu.make_async_remote_copy(
            src_ref=cleaned.at[whole_of(e, 1 - chip), at], dst_ref=early_in.at[e, at],
            send_sem=early_send.at[i], recv_sem=early_recv.at[i],
            device_id=device(1 - chip, core), device_id_type=MESH,
        )

    def start_early(step):
        low, high = ((0,) + marks)[step : step + 2]
        for i in range(low, high):
            send_early(i).start()

    each_load(jnp.int32(0), lambda c: c.start())

    barrier = pltpu.get_barrier_semaphore()
    for d in range(1, n_mz):
        pl.semaphore_signal(barrier, inc=1, device_id=at_z(d), device_id_type=MESH)
    for d in range(1, n_pix):
        pl.semaphore_signal(barrier, inc=1, device_id=at_pix(d), device_id_type=MESH)

    taps = k_ref.shape[0]
    line[...] = jnp.zeros_like(line)
    line[:, :taps] = k_ref[...].astype(jnp.float32).reshape(1, taps)
    base = jnp.broadcast_to(line[...], (OUT, WIN))
    band = pltpu.roll(base, LANES - taps // 2, 1, stride=1, stride_axis=0)
    full_band = band.T.astype(jnp.bfloat16)
    w_ref[...] = full_band[LANES : LANES + OUT]
    low = lax.broadcasted_iota(jnp.int32, (LANES, LANES), 0) < LANES // 2
    corner = jnp.where(low, full_band[WIN - LANES :, OUT - LANES :], full_band[:LANES, :LANES])
    edge_ref[...] = jnp.zeros_like(edge_ref)
    edge_ref[:LANES, :LANES] = corner
    edge_ref[LANES:, LANES:] = corner
    total[...] = jnp.zeros_like(total)
    for pos in range(1, min(slots, tiles)):
        each_load(jnp.int32(pos), lambda c: c.start())

    to_right = pltpu.make_async_remote_copy(
        src_ref=spectra.at[:, pl.ds(bins - LANES, LANES)], dst_ref=halo.at[0],
        send_sem=halo_send.at[0], recv_sem=halo_recv.at[0],
        device_id=at_z(1), device_id_type=MESH,
    )
    to_left = pltpu.make_async_remote_copy(
        src_ref=spectra.at[:, pl.ds(0, LANES)], dst_ref=halo.at[1],
        send_sem=halo_send.at[1], recv_sem=halo_recv.at[1],
        device_id=at_z(n_mz - 1), device_id_type=MESH,
    )

    @pl.when(mz == 0)
    def _():
        halo[0] = jnp.zeros(halo.shape[1:], halo.dtype)

    @pl.when(mz == n_mz - 1)
    def _():
        halo[1] = jnp.zeros(halo.shape[1:], halo.dtype)

    def clean(pos):
        slot = lax.rem(pos, slots)
        at = tile_of(pos)
        each_load(pos, lambda c: c.wait())

        @pl.when(pos == tiles - 2)
        def _():
            @pl.when(mz > 0)
            def _():
                to_right.wait_recv()

            raw[slot, :, :LANES] = halo[0]

        @pl.when(pos == tiles - 1)
        def _():
            @pl.when(mz < n_mz - 1)
            def _():
                to_left.wait_recv()

            raw[slot, :, tile + LANES :] = halo[1]

        w, edge = w_ref[...], edge_ref[...]
        low = lax.broadcasted_iota(jnp.int32, (raw.shape[1], LANES), 1) < LANES // 2
        block = lambda i: raw[slot, :, LANES + i * LANES : LANES + (i + 1) * LANES]
        group = 4
        ready, added = [], None

        def sketch_part(js, added):
            begin, end = js[0] * OUT, (js[-1] + 1) * OUT
            step = min(width, end - begin)
            pieces = [
                cleaned[at * per + i // width, :, i % width : i % width + step]
                for i in range(begin, end, step)
            ]
            one = jnp.dot(
                jnp.concatenate(pieces, axis=1), tap[slot, begin:end],
                preferred_element_type=jnp.float32,
            )
            return one if added is None else added + one

        for j in range(0, tile // OUT, 2):
            sides = [jnp.where(low, block(2 * k + 2), block(2 * k - 1)) for k in (j, j + 1)]
            outer = jnp.dot(
                jnp.concatenate(sides, axis=1), edge, preferred_element_type=jnp.float32
            )
            for k in (j, j + 1):
                mine = raw[slot, :, LANES + k * OUT : LANES + (k + 1) * OUT]
                inner = jnp.dot(mine, w, preferred_element_type=jnp.float32)
                side = outer[:, (k - j) * LANES : (k - j + 1) * LANES]
                smooth = inner + jnp.concatenate(
                    [jnp.where(low, side, 0.0), jnp.where(low, 0.0, side)], axis=1
                )
                one = (mine.astype(jnp.float32) - smooth).astype(jnp.bfloat16)
                piece, inside = (k * OUT) // width, (k * OUT) % width
                cleaned[at * per + piece, :, inside : inside + OUT] = one
            ready += [j, j + 1]
            if len(ready) >= 2 * group:
                added = sketch_part(ready[:group], added)
                ready = ready[group:]
        while ready:
            added = sketch_part(ready[:group], added)
            ready = ready[group:]
        total[...] += added

    @pl.loop(0, tiles)
    def _(pos):
        @pl.when(pos == met)
        def _():
            pl.semaphore_wait(barrier, n_mz - 1 + n_pix - 1)

            @pl.when(mz < n_mz - 1)
            def _():
                to_right.start()

            @pl.when(mz > 0)
            def _():
                to_left.start()

            start_early(0)

        clean(pos)

        @pl.when(pos + slots < tiles)
        def _():
            each_load(pos + slots, lambda c: c.start())

    @pl.when(mz < n_mz - 1)
    def _():
        to_right.wait_send()

    @pl.when(mz > 0)
    def _():
        to_left.wait_send()

    rows = parts.shape[1]
    for z in range(n_mz):
        parts[z] = total[z * rows : (z + 1) * rows]

    def scatter(d):
        return pltpu.make_async_remote_copy(
            src_ref=parts.at[lax.rem(mz + d, n_mz)], dst_ref=parts_in.at[d - 1],
            send_sem=parts_send.at[d - 1], recv_sem=parts_recv.at[d - 1],
            device_id=at_z(d), device_id_type=MESH,
        )

    for d in range(1, n_mz):
        scatter(d).start()
    start_early(1)
    mine = parts[mz]
    for d in range(1, n_mz):
        scatter(d).wait_recv()
        mine = mine + parts_in[d - 1]
    sketch[mz] = mine

    def gather(d, owner):
        return pltpu.make_async_remote_copy(
            src_ref=sketch.at[mz], dst_ref=sketch.at[owner],
            send_sem=all_send.at[d - 1], recv_sem=all_recv.at[d - 1],
            device_id=at_z(d), device_id_type=MESH,
        )

    for d in range(1, n_mz):
        gather(d, mz).start()
    start_early(2)
    for d in range(1, n_mz):
        gather(d, lax.rem(mz + n_mz - d, n_mz)).wait_recv()
    sk = jnp.concatenate([sketch[z] for z in range(n_mz)], axis=0)

    square = lax.dot_general(
        sk, sk, (((0,), (0,)), ((), ())), precision=HIGHEST, preferred_element_type=jnp.float32
    )
    size = square.shape[0]
    top, strip = size // 2, size // 4
    gram[:top] = square[:top]
    left = lax.broadcasted_iota(jnp.int32, (strip, size), 1) < top
    gram[top:] = jnp.where(
        left, pltpu.roll(square[top : top + strip], top, 1), square[top + strip :]
    )

    def share_gram(d):
        return pltpu.make_async_remote_copy(
            src_ref=gram, dst_ref=gram_in.at[d - 1],
            send_sem=gram_send.at[d - 1], recv_sem=gram_recv.at[d - 1],
            device_id=device(chip_of(d), core), device_id_type=MESH,
        )

    relay = pltpu.make_async_remote_copy(
        src_ref=gram_sum, dst_ref=gram_in.at[chips - 1],
        send_sem=gram_send.at[chips - 1], recv_sem=gram_recv.at[chips - 1],
        device_id=device(chip, other), device_id_type=MESH,
    )

    for d in range(1, chips):
        share_gram(d).start()
    to_far = pltpu.make_async_remote_copy(
        src_ref=flat, dst_ref=flat_far, send_sem=far_send.at[0], recv_sem=far_recv.at[0],
        device_id=device(1 - chip, core), device_id_type=MESH,
    )
    full = gram[...]
    for d in range(1, chips):
        share_gram(d).wait_recv()
        full = full + gram_in[d - 1]
    gram_sum[...] = full
    relay.start()
    relay.wait_recv()
    full = full + gram_in[chips - 1]
    if early:
        start_early(3)
    full = full * (1.0 / pixels)
    total[:top] = full[:top]
    total[top : top + strip] = pltpu.roll(full[top:], top, 1)
    total[top + strip :] = full[top:]
    whiten(total, x_ref)
    x = x_ref[...]
    by_lane = (((1,), (1,)), ((), ()))

    def fill(target, source):
        basis_t = source[...].reshape(n_pix, share, source.shape[1])
        for chunk in range(n_pix):
            d = lax.rem(chunk // 2 - chip + chips, chips)
            at = d * share + jnp.where(core == chunk % 2, half, 0)
            target[pl.ds(pl.multiple_of(at, share), share), :] = basis_t[chunk]

    flat[...] = lax.dot_general(
        x, sk, by_lane, precision=HIGHEST, preferred_element_type=jnp.float32
    ).astype(jnp.bfloat16)
    if early:
        to_far.start()
    fill(lhs, flat)

    def to_core(k):
        return pltpu.make_async_remote_copy(
            src_ref=give.at[lax.rem(k, ring)], dst_ref=core_in.at[k],
            send_sem=give_sem.at[lax.rem(k, ring)], recv_sem=core_sem.at[k],
            device_id=device(chip, other), device_id_type=MESH,
        )

    def to_chip(d, k):
        return pltpu.make_async_remote_copy(
            src_ref=x_give.at[d - 1, k], dst_ref=x_in.at[d - 1, k],
            send_sem=x_send_sem.at[d - 1, k], recv_sem=x_recv_sem.at[d - 1, k],
            device_id=device(chip_of(d), core), device_id_type=MESH,
        )

    def product(left, right):
        part = jnp.dot(left, right, preferred_element_type=jnp.float32) * factor
        return part.astype(jnp.bfloat16)

    def first(i, alone):
        slot = lax.rem(i, ring)

        @pl.when(i >= ring)
        def _():
            to_core(i - ring).wait_send()

        part = product(lhs[...], cleaned[chunk_of(i)])
        if alone:
            for piece in range(PIECES):
                send_early((i - both) * PIECES + piece).wait_recv()
            far = product(lhs_far[...], early_in[i - both])
            part = (part.astype(jnp.float32) + far.astype(jnp.float32)).astype(jnp.bfloat16)
        give[slot] = part[:half]
        to_core(i).start()
        hold[slot] = part[half:]

    def second(i):
        to_core(i).wait_recv()
        slot = lax.rem(i, ring)
        k = chunk_of(i)
        added = hold[slot].astype(jnp.float32) + core_in[i].astype(jnp.float32)
        acc[k] = added[:share]
        for d in range(1, chips):
            x_give[d - 1, k] = added[d * share : (d + 1) * share].astype(jnp.bfloat16)
            to_chip(d, k).start()

    def emit(k, value):
        out[:, pl.ds(pl.multiple_of(k * width, width), width)] = value.astype(jnp.bfloat16)

    lag = min(LAG, ring - 1, both)
    mine = chunks - early

    @pl.loop(0, lag)
    def _(i):
        first(i, False)

    @pl.loop(lag, both)
    def _(i):
        first(i, False)
        second(i - lag)

    basis[...] = lax.dot_general(
        sk, x, by_lane, precision=HIGHEST, preferred_element_type=jnp.float32
    ).astype(jnp.bfloat16)

    if early:
        to_far.wait_recv()
        fill(lhs_far, flat_far)

        @pl.loop(both, mine)
        def _(i):
            first(i, True)
            second(i - lag)

    @pl.loop(mine - lag, mine)
    def _(i):
        second(i)

    @pl.loop(max(mine - ring, 0), mine)
    def _(i):
        to_core(i).wait_send()

    for d in range(1, n_mz):
        scatter(d).wait_send()
        gather(d, mz).wait_send()
    for d in range(1, chips):
        share_gram(d).wait_send()
    relay.wait_send()
    if early:
        to_far.wait_send()
        for i in range(early * PIECES):
            send_early(i).wait_send()

        @pl.loop(0, early)
        def _(e):
            emit(whole_of(e, chip), acc[whole_of(e, chip)])

    @pl.loop(0, both)
    def _(i):
        k = chunk_of(i)
        added = acc[k]
        for d in range(1, chips):
            to_chip(d, k).wait()
            added = added + x_in[d - 1, k].astype(jnp.float32)
        emit(k, added)

    if early:
        @pl.loop(0, early)
        def _(e):
            k = whole_of(e, 1 - chip)
            to_chip(1, k).wait_recv()
            emit(k, x_in[0, k])
            to_chip(1, whole_of(e, chip)).wait_send()


def per_device(spectra, kernel, probes):
    rows, bins = spectra.shape
    cols = probes.shape[1]
    n_pix, n_mz = lax.axis_size("pix"), lax.axis_size("mz")
    pixels = rows * n_pix
    factor = 1.0 / math.sqrt(float(pixels))
    share = cols // n_pix
    chips = n_pix // 2
    half = chips * share
    tile = min(4096, bins // 2)
    width = min(2048, tile)
    chunks = bins // width
    slots, ring = 3, 4
    fits = chips == 2 and tile % width == 0 and bins // tile >= 8
    early, marks = (EARLY, MARKS) if fits else (0, (0, 0, 0, 0))
    kept = max(early, 1)
    away = max(chips - 1, 1)
    part = rows // n_mz
    bf16, f32 = jnp.bfloat16, jnp.float32
    dma = pltpu.SemaphoreType.DMA
    held = pl.pallas_call(
        functools.partial(fused_kernel, n_mz, n_pix, factor, float(pixels), early, marks),
        in_specs=[
            pl.BlockSpec(memory_space=pl.ANY),
            pl.BlockSpec(memory_space=pltpu.VMEM),
            pl.BlockSpec(memory_space=pl.ANY),
        ],
        out_specs=[pl.BlockSpec(memory_space=pltpu.VMEM), pl.BlockSpec(memory_space=pltpu.VMEM)],
        out_shape=[
            pltpu.VMEM((rows, cols), bf16),
            pltpu.VMEM((share, bins), bf16),
        ],
        scratch_shapes=[
            pltpu.VMEM((slots, rows, tile + 2 * LANES), bf16),
            pltpu.VMEM((slots, tile, cols), bf16),
            pltpu.VMEM((1, WIN), f32),
            pltpu.VMEM((OUT, OUT), bf16),
            pltpu.VMEM((OUT, OUT), bf16),
            pltpu.VMEM((2, rows, LANES), bf16),
            pltpu.VMEM((chunks, rows, width), bf16),
            pltpu.VMEM((rows, cols), f32),
            pltpu.VMEM((n_mz, part, cols), f32),
            pltpu.VMEM((n_mz - 1, part, cols), f32),
            pltpu.VMEM((n_mz, part, cols), f32),
            pltpu.VMEM((cols // 4 * 3, cols), f32),
            pltpu.VMEM((cols // 4 * 3, cols), f32),
            pltpu.VMEM((chips, cols // 4 * 3, cols), f32),
            pltpu.VMEM((cols, cols), f32),
            pltpu.VMEM((cols, rows), bf16),
            pltpu.VMEM((ring, half, width), bf16),
            pltpu.VMEM((chunks, half, width), bf16),
            pltpu.VMEM((ring, half, width), bf16),
            pltpu.VMEM((away, chunks, share, width), bf16),
            pltpu.VMEM((away, chunks, share, width), bf16),
            pltpu.VMEM((chunks, share, width), f32),
            pltpu.VMEM((cols, rows), bf16),
            pltpu.VMEM((kept, rows, width), bf16),
            pltpu.VMEM((cols, rows), bf16),
            pltpu.VMEM((cols, rows), bf16),
            dma((slots,)),
            dma((slots,)),
            dma((2,)),
            dma((2,)),
            dma((n_mz - 1,)),
            dma((n_mz - 1,)),
            dma((n_mz - 1,)),
            dma((n_mz - 1,)),
            dma((chips,)),
            dma((chips,)),
            dma((ring,)),
            dma((chunks,)),
            dma((away, chunks)),
            dma((away, chunks)),
            dma((kept * PIECES,)),
            dma((kept * PIECES,)),
            dma((1,)),
            dma((1,)),
        ],
        compiler_params=pltpu.CompilerParams(
            collective_id=0, has_side_effects=True, vmem_limit_bytes=58 * 2**20
        ),
        cost_estimate=pl.CostEstimate(
            flops=2 * rows * bins * (WIN + 2 * cols),
            bytes_accessed=2 * bins * (rows + cols + share),
            transcendentals=0,
        ),
    )(spectra, kernel, probes)
    return pl.pallas_call(
        write_kernel,
        in_specs=[pl.BlockSpec(memory_space=pltpu.VMEM)] * 2,
        out_specs=[pl.BlockSpec(memory_space=pl.ANY)] * 2,
        out_shape=[
            jax.ShapeDtypeStruct((rows, cols), bf16),
            jax.ShapeDtypeStruct((share, bins), bf16),
        ],
        scratch_shapes=[dma((2,))],
        compiler_params=pltpu.CompilerParams(vmem_limit_bytes=2**20),
    )(*[pltpu.with_memory_space_constraint(one, pltpu.VMEM) for one in held])


def solution(mesh):
    in_specs = (P(("groups", "pix"), "mz"), P(), P("mz", None))
    out_specs = (P(("groups", "pix"), None), P(("groups", "pix"), "mz"))
    return jax.shard_map(
        per_device, mesh=mesh, in_specs=in_specs, out_specs=out_specs, check_vma=False
    )
```
